32 devices in a mesh: gx: 4 (over y, x), gy: 2 (over core), gz: 4 (over z).
Axes of the slice: x: 2, y: 2, z: 4, core: 2. Of those that a mesh axis runs over, the one named last changes fastest.
Arguments:
- features: bfloat16 [32, 32, 64, 512], P(None, 'gx', 'gy', 'gz'), may hold values from -12 to 12
- posteriors: bfloat16 [16, 32, 64, 512], P(None, 'gx', 'gy', 'gz'), may hold values from 0 to 1, as said below
Outputs:
- segmentation: bfloat16 [16, 32, 64, 512], P(None, 'gx', 'gy', 'gz')
- class_means: float32 [16, 32], replicated
The draws below stay inside these ranges and needn't reach their ends.
Inputs may be any that keep to these rules, and one draw needn't show every extreme that they name: Each voxel's 16 initial posteriors are positive and sum to one up to rounding.
All inputs are finite; a program needn't handle non-finite values.
Results may differ from the reference program's by a relative error of at most 0.0075.
Values may be sent and summed in bfloat16 or wider, within the bound.
No kernel may reach another device: no remote copies, remote signals or barrier semaphores. Data moves between devices by JAX's collectives and lax.ppermute only.
A program may use at most 128 MiB of HBM per device.

```python
import jax
import jax.numpy as jnp
from jax import lax

FEATS = 32
CLASSES = 16
SWEEPS = 2
VOXELS_ALONG_X = 32
VOXELS_ALONG_Y = 64
VOXELS_ALONG_Z = 512


def class_labels(key):
    grid_shape = (VOXELS_ALONG_X, VOXELS_ALONG_Y, VOXELS_ALONG_Z)
    share = CLASSES // 4
    order = jax.random.permutation(jax.random.fold_in(key, 5), CLASSES).astype(jnp.int32)
    quarter = (jnp.arange(VOXELS_ALONG_X, dtype=jnp.int32) * 4 // VOXELS_ALONG_X)[:, None, None]
    eighth = (jnp.arange(VOXELS_ALONG_Z, dtype=jnp.int32) * 8 // VOXELS_ALONG_Z)[None, None, :]
    pick = jax.random.randint(jax.random.fold_in(key, 7), grid_shape, 0, share).astype(jnp.int32)
    coin = jax.random.randint(jax.random.fold_in(key, 8), grid_shape, 0, 2).astype(jnp.int32)
    pick = jnp.where(coin == 1, eighth % share + 0 * pick, pick)
    slot = quarter * share + pick
    return jnp.take(order, slot)


def draw_features(key, part):
    label = class_labels(key)
    centers = 1.2 * jax.random.normal(jax.random.fold_in(key, 11), (FEATS, CLASSES), jnp.float32)
    base = jnp.take(centers, label, axis=1)
    noise = jax.random.normal(jax.random.fold_in(key, 12), (FEATS, VOXELS_ALONG_X, VOXELS_ALONG_Y, VOXELS_ALONG_Z), jnp.float32)
    return jnp.clip(base + noise, -12.0, 12.0).astype(jnp.bfloat16)


def draw_posteriors(key, part):
    label = class_labels(key)
    onehot = (label[None] == jnp.arange(CLASSES, dtype=jnp.int32)[:, None, None, None]).astype(jnp.float32)
    noise = jax.random.normal(jax.random.fold_in(key, 14), (CLASSES, VOXELS_ALONG_X, VOXELS_ALONG_Y, VOXELS_ALONG_Z), jnp.float32)
    return jax.nn.softmax(1.5 * onehot + noise, axis=0).astype(jnp.bfloat16)


def setup_inputs(seed: int = 0) -> dict:
    streams_of = jax.random.split(jax.random.key(seed), 3)
    features = draw_features(jax.random.fold_in(streams_of[2], 71), 0)
    posteriors = draw_posteriors(jax.random.fold_in(streams_of[2], 71), 0)
    return {"features": features, "posteriors": posteriors}


beta_coupling = 1.0
ridge = 0.1

def finish(counts, total_weight, first_moment, scatter):
    identity = jnp.eye(first_moment.shape[1], dtype=jnp.float32)
    centers = first_moment / counts[:, None]
    spread = scatter / counts[:, None, None] - centers[:, :, None] * centers[:, None, :] + ridge * identity
    factor = jnp.linalg.cholesky(spread)
    whiten = jax.vmap(lambda lower_factor: jax.scipy.linalg.solve_triangular(lower_factor, identity, lower=True))(factor)
    offset = jnp.einsum('kgf,kf->kg', whiten, centers, precision=lax.Precision.HIGHEST)
    biases = jnp.log(counts / total_weight) - jnp.sum(jnp.log(jnp.diagonal(factor, axis1=1, axis2=2)), axis=1)
    return (centers, whiten, offset, biases)

def local_moments(posterior, voxels):
    flat_post = posterior.reshape(posterior.shape[0], -1)
    flat_vox = voxels.reshape(voxels.shape[0], -1)
    contract = (((1,), (1,)), ((), ()))
    counts = jnp.sum(flat_post.astype(jnp.float32), axis=1)
    first_moment = lax.dot_general(flat_post.astype(jnp.float32), flat_vox.astype(jnp.float32), contract, preferred_element_type=jnp.float32)

    def second(weights_row):
        weighted = weights_row[None, :] * flat_vox
        return lax.dot_general(weighted.astype(jnp.float32), flat_vox.astype(jnp.float32), contract, preferred_element_type=jnp.float32)
    scatter = lax.map(second, flat_post)
    return (counts, first_moment, scatter)

def loglik(voxels, whiten, offset, biases):
    flat_vox = voxels.reshape(voxels.shape[0], -1)
    rounded = whiten.astype(jnp.bfloat16)

    def per_class(class_record):
        matrix, shift, level = class_record
        whitened = jnp.dot(matrix.astype(jnp.float32), flat_vox.astype(jnp.float32), preferred_element_type=jnp.float32) - shift[:, None]
        return level - 0.5 * jnp.sum(whitened * whitened, axis=0)
    scores = lax.map(per_class, (rounded, offset, biases))
    return scores.reshape((whiten.shape[0],) + voxels.shape[1:])

def neighbours(padded):
    inner = padded[:, 2:, 1:-1, 1:-1] + padded[:, :-2, 1:-1, 1:-1]
    inner = inner + padded[:, 1:-1, 2:, 1:-1] + padded[:, 1:-1, :-2, 1:-1]
    return inner + padded[:, 1:-1, 1:-1, 2:] + padded[:, 1:-1, 1:-1, :-2]

def state_update(scores, near_sum):
    return jax.nn.softmax(scores + beta_coupling * near_sum, axis=0).astype(jnp.bfloat16)

def padded_of(posterior):
    return jnp.pad(posterior.astype(jnp.float32), ((0, 0), (1, 1), (1, 1), (1, 1)))

def reference(features, posteriors):
    counts, first_moment, scatter = local_moments(posteriors, features)
    centers, whiten, offset, biases = finish(counts, jnp.sum(counts), first_moment, scatter)
    scores = loglik(features, whiten, offset, biases)
    current = posteriors
    for pass_index in range(SWEEPS):
        current = state_update(scores, neighbours(padded_of(current)))
    counts, first_moment, scatter = local_moments(current, features)
    centers, whiten, offset, biases = finish(counts, jnp.sum(counts), first_moment, scatter)
    scores = loglik(features, whiten, offset, biases)
    segmentation = state_update(scores, neighbours(padded_of(current)))
    return (segmentation, centers)
```

```python
import functools

import jax
import jax.numpy as jnp
from jax import lax
from jax.experimental import pallas as pl
from jax.experimental.pallas import tpu as pltpu
from jax.sharding import PartitionSpec as P

BETA = 1.0
RIDGE = 0.1
AXES = ("gx", "gy", "gz")
ROWS_ROWS = (((1,), (1,)), ((), ()))
VMEM_BYTES = 60 * 2**20
f32, bf16 = jnp.float32, jnp.bfloat16


def lane_iota(shape):
    return lax.broadcasted_iota(jnp.int32, shape, len(shape) - 1)


def moments_of(x, q):
    ny = x.shape[0]
    xs = jnp.concatenate([x[y] for y in range(ny)], axis=1)
    qs = jnp.concatenate([q[y] for y in range(ny)], axis=1)
    weighted = jnp.concatenate([xs[f : f + 1] * qs for f in range(xs.shape[0])], axis=0)
    ones = jnp.ones((16, xs.shape[1]), bf16)
    scatter = lax.dot_general(xs, weighted, ROWS_ROWS, preferred_element_type=f32)
    first = lax.dot_general(
        qs, jnp.concatenate([xs, ones], axis=0), ROWS_ROWS, preferred_element_type=f32
    )
    return scatter, first


def add_moments(out_ref, x, q, start):
    scatter, first = moments_of(x, q)
    feats, lanes = scatter.shape
    pieces = [scatter[:, j : j + 128] for j in range(0, lanes, 128)]
    first = jnp.pad(first, ((0, 0), (0, 128 - first.shape[1])))
    all_of = jnp.concatenate(pieces + [first], axis=0)

    @pl.when(start)
    def _():
        out_ref[...] = all_of

    @pl.when(jnp.logical_not(start))
    def _():
        out_ref[...] += all_of


def m_step(total_ref, w_ref, bias_ref):
    classes = bias_ref.shape[0]
    feats = w_ref.shape[0] // classes
    per = 128 // classes
    first = total_ref[pl.ds(total_ref.shape[0] - classes, classes), :]
    lane = lane_iota((classes, 128))
    counts = jnp.broadcast_to(first[:, feats : feats + 1], (classes, 128))
    inv = 1.0 / counts
    means = first / counts
    shifted = pltpu.roll(means, feats, 1)
    inside = (lane >= feats) & (lane < 2 * feats)
    rows = []
    for t in range(feats // per):
        block = total_ref[pl.ds(t * feats, feats), :]
        wide = jnp.concatenate(
            [jnp.zeros((feats, 128), f32), block, jnp.zeros((128 - 2 * feats, 128), f32)], axis=0
        )
        turned = wide.T
        for s in range(per):
            f = t * per + s
            mean_f = jnp.broadcast_to(means[:, f : f + 1], (classes, 128))
            spread = turned[s * classes : (s + 1) * classes] * inv - mean_f * shifted
            spread = spread + jnp.where(lane == feats + f, RIDGE, 0.0)
            rest = jnp.where(lane == 2 * feats, mean_f, jnp.where(lane == f, 1.0, 0.0))
            rows.append(jnp.where(inside, spread, rest))
    logdet = jnp.zeros((classes, 128), f32)
    for p in range(feats):
        row = rows[p]
        pivot = jnp.broadcast_to(row[:, feats + p : feats + p + 1], (classes, 128))
        scaled = row * (1.0 / pivot)
        for i in range(p + 1, feats):
            factor = jnp.broadcast_to(row[:, feats + i : feats + i + 1], (classes, 128))
            rows[i] = rows[i] - factor * scaled
        logdet = logdet + jnp.log(pivot)
        white = row * lax.rsqrt(pivot)
        shift = -jnp.broadcast_to(white[:, 2 * feats : 2 * feats + 1], (classes, 128))
        high = shift.astype(bf16).astype(f32)
        middle = (shift - high).astype(bf16).astype(f32)
        low = shift - high - middle
        parts = jnp.where(
            lane == feats, high, jnp.where(lane == feats + 1, middle, jnp.where(lane == feats + 2, low, 0.0))
        )
        white = jnp.where(lane < feats, white, parts)
        w_ref[pl.ds(p * classes, classes), :] = white[:, : feats + 16].astype(bf16)
    total = jnp.sum(counts, axis=0, keepdims=True)
    bias_ref[...] = jnp.log(counts / total) - 0.5 * logdet
    return means


def loglik_of(x, w_ref, bias):
    n, feats, nz = x.shape
    classes = bias.shape[0]
    xs = jnp.concatenate([x[j] for j in range(n)], axis=1)
    xs = jnp.concatenate([xs, jnp.ones((16, n * nz), bf16)], axis=0)
    white = jnp.dot(w_ref[...], xs, preferred_element_type=f32)
    white = white * white
    square = white[:classes]
    for g in range(1, feats):
        square = square + white[g * classes : (g + 1) * classes]
    return jnp.stack(
        [bias[:, :nz] - 0.5 * square[:, j * nz : (j + 1) * nz] for j in range(n)], axis=0
    )


def shift_matrix(ny, nz):
    src = lax.broadcasted_iota(jnp.int32, (nz + 128, nz), 0)
    dst = lax.broadcasted_iota(jnp.int32, (nz + 128, nz), 1)
    near = (src < nz) & ((src == dst + 1) | (src == dst - 1))
    face = src - nz
    high = (face >= 0) & (face < ny) & (dst == nz - 1)
    low = (face >= ny) & (face < 2 * ny) & (dst == 0)
    return jnp.where(near | high | low, 1.0, 0.0).astype(bf16)


def take_matrix(ny, nz):
    src = lax.broadcasted_iota(jnp.int32, (nz, 128), 0)
    dst = lax.broadcasted_iota(jnp.int32, (nz, 128), 1)
    hit = ((src == 0) & (dst < ny)) | ((src == nz - 1) & (dst >= ny) & (dst < 2 * ny))
    return jnp.where(hit, 1.0, 0.0).astype(bf16)


def own_lane(ny, classes):
    lane = lane_iota((ny, classes, 128))
    y = lax.broadcasted_iota(jnp.int32, (ny, classes, 128), 0)
    return (lane == y) | (lane == ny + y)


def near_of(i, nx, q_ref, x_before, x_after, y_before, y_after, z_before, z_after, flags):
    ny, classes, nz = q_ref.shape[1:]
    mid = q_ref[i]
    down = jnp.where(i > 0, q_ref[jnp.maximum(i - 1, 0)], x_before[...]).astype(f32)
    up = jnp.where(i < nx - 1, q_ref[jnp.minimum(i + 1, nx - 1)], x_after[...]).astype(f32)
    mid32 = mid.astype(f32)
    first = y_before[pl.ds(i, 1)].astype(f32) * flags[0]
    last = y_after[pl.ds(i, 1)].astype(f32) * flags[1]
    left = jnp.concatenate([first, mid32[:-1]], axis=0)
    right = jnp.concatenate([mid32[1:], last], axis=0)
    lane = lane_iota((classes, 128))
    face = jnp.where(lane < ny, z_after[i].astype(f32), z_before[i].astype(f32))
    face = jnp.where(own_lane(ny, classes), face[None], 0.0).astype(bf16)
    both = jnp.concatenate([mid, face], axis=2).reshape(ny * classes, nz + 128)
    along = jnp.dot(both, shift_matrix(ny, nz), preferred_element_type=f32)
    return (down + up) + (left + right) + along.reshape(ny, classes, nz)


def update_of(scores, near):
    s = scores + BETA * near
    e = jnp.exp(s - jnp.max(s, axis=1, keepdims=True))
    return (e * (1.0 / jnp.sum(e, axis=1, keepdims=True))).astype(bf16)


def put_faces(i, nx, q, xlo, xhi, yface, zface):
    ny, classes, nz = q.shape

    @pl.when(i == 0)
    def _():
        xlo[...] = q

    @pl.when(i == nx - 1)
    def _():
        xhi[...] = q

    yface[0, pl.ds(i, 1)] = q[0:1]
    yface[1, pl.ds(i, 1)] = q[ny - 1 : ny]
    spread = jnp.dot(q.reshape(ny * classes, nz), take_matrix(ny, nz), preferred_element_type=f32)
    spread = jnp.where(own_lane(ny, classes), spread.reshape(ny, classes, 128), 0.0)
    zface[pl.ds(i, 1)] = jnp.sum(spread, axis=0, keepdims=True).astype(bf16)


def first_kernel(x_ref, q_ref, xt, qt, xlo, xhi, yface, zface, mom):
    nx = x_ref.shape[1]

    def slab(i, carry):
        x = jnp.swapaxes(x_ref[:, i], 0, 1)
        q = jnp.swapaxes(q_ref[:, i], 0, 1)
        xt[i] = x
        qt[i] = q
        put_faces(i, nx, q, xlo, xhi, yface, zface)
        add_moments(mom, x, q, i == 0)
        return carry

    lax.fori_loop(0, nx, slab, 0)


def second_kernel(flags_ref, total, xt, qt, xb, xa, yb, ya, zb, za, sc, q1, xlo, xhi, yface, zface, w, bias):
    nx = xt.shape[0]
    m_step(total, w, bias)
    flags = (flags_ref[0], flags_ref[1])

    def slab(i, carry):
        half = xt.shape[1] // 2
        sc[i, pl.ds(0, half)] = loglik_of(xt[i, pl.ds(0, half)], w, bias[...])
        sc[i, pl.ds(half, half)] = loglik_of(xt[i, pl.ds(half, half)], w, bias[...])
        q = update_of(sc[i], near_of(i, nx, qt, xb, xa, yb, ya, zb, za, flags))
        q1[i] = q
        put_faces(i, nx, q, xlo, xhi, yface, zface)
        return carry

    lax.fori_loop(0, nx, slab, 0)


def third_kernel(flags_ref, sc, xt, qt, xb, xa, yb, ya, zb, za, q2, xlo, xhi, yface, zface, mom):
    nx = xt.shape[0]
    flags = (flags_ref[0], flags_ref[1])

    def slab(i, carry):
        q = update_of(sc[i], near_of(i, nx, qt, xb, xa, yb, ya, zb, za, flags))
        q2[i] = q
        put_faces(i, nx, q, xlo, xhi, yface, zface)
        add_moments(mom, xt[i], q, i == 0)
        return carry

    lax.fori_loop(0, nx, slab, 0)


def fourth_kernel(flags_ref, total, xt, qt, xb, xa, yb, ya, zb, za, seg, means_ref, w, bias):
    nx = xt.shape[0]
    means = m_step(total, w, bias)
    means_ref[...] = means[:, : means_ref.shape[1]]
    flags = (flags_ref[0], flags_ref[1])

    def slab(i, carry):
        half = xt.shape[1] // 2
        scores = jnp.concatenate(
            [loglik_of(xt[i, pl.ds(j * half, half)], w, bias[...]) for j in range(2)], axis=0
        )
        q = update_of(scores, near_of(i, nx, qt, xb, xa, yb, ya, zb, za, flags))
        seg[:, i] = jnp.swapaxes(q, 0, 1)
        return carry

    lax.fori_loop(0, nx, slab, 0)


def sum_over_devices(x):
    for axis in ("gy", "gx", "gz"):
        n = lax.axis_size(axis)
        step = 1
        if n & (n - 1):
            x = lax.psum(x, axis)
            continue
        while step < n:
            x = x + lax.ppermute(x, axis, [(i, i ^ step) for i in range(n)])
            step *= 2
    return x


def exchange(xlo, xhi, yface, zface):
    def shift(value, axis, up):
        n = lax.axis_size(axis)
        pairs = [(i, i + 1) for i in range(n - 1)]
        return lax.ppermute(value, axis, pairs if up else [(j, i) for i, j in pairs])

    xb, xa = shift(xhi, "gx", True), shift(xlo, "gx", False)
    if lax.axis_size("gy") == 2:
        other = lax.ppermute(yface, "gy", [(0, 1), (1, 0)])
        yb, ya = other[1], other[0]
    else:
        yb, ya = shift(yface[1], "gy", True), shift(yface[0], "gy", False)
    zb, za = shift(zface, "gz", True), shift(zface, "gz", False)
    return xb, xa, yb, ya, zb, za


def call(kernel, outs, scratch, smem, *args):
    vmem = pl.BlockSpec(memory_space=pltpu.VMEM)
    specs = [pl.BlockSpec(memory_space=pltpu.SMEM)] * smem + [vmem] * (len(args) - smem)
    return pl.pallas_call(
        kernel,
        out_shape=tuple(outs),
        in_specs=specs,
        out_specs=tuple(vmem for _ in outs),
        scratch_shapes=scratch,
        compiler_params=pltpu.CompilerParams(vmem_limit_bytes=VMEM_BYTES),
    )(*args)


def local(features, posteriors):
    feats, nx, ny, nz = features.shape
    classes = posteriors.shape[0]
    shape = jax.ShapeDtypeStruct
    brick = shape((nx, ny, classes, nz), bf16)
    faces = [
        shape((ny, classes, nz), bf16),
        shape((ny, classes, nz), bf16),
        shape((2, nx, classes, nz), bf16),
        shape((nx, classes, 128), bf16),
    ]
    mom = shape((feats * feats * classes // 128 + classes, 128), f32)
    solved = [pltpu.VMEM((feats * classes, feats + 16), bf16), pltpu.VMEM((classes, 128), f32)]
    at, n = lax.axis_index("gy"), lax.axis_size("gy")
    flags = jnp.stack([at > 0, at < n - 1]).astype(f32)

    xt, qt, *edge, part = call(
        first_kernel, [shape((nx, ny, feats, nz), bf16), brick, *faces, mom], [], 0, features, posteriors
    )
    total = sum_over_devices(part)
    halo = exchange(*edge)
    sc, q1, *edge = call(
        second_kernel, [shape((nx, ny, classes, nz), f32), brick, *faces], solved, 1, flags, total, xt, qt, *halo
    )
    halo = exchange(*edge)
    q2, *edge, part = call(third_kernel, [brick, *faces, mom], [], 1, flags, sc, xt, q1, *halo)
    total = sum_over_devices(part)
    halo = exchange(*edge)
    return call(
        fourth_kernel,
        [shape(posteriors.shape, bf16), shape((classes, feats), f32)],
        solved,
        1,
        flags,
        total,
        xt,
        q2,
        *halo,
    )


def solution(mesh):
    placed = P(None, "gx", "gy", "gz")
    return jax.shard_map(
        local, mesh=mesh, in_specs=(placed, placed), out_specs=(placed, P()), check_vma=False
    )
```

```python
import jax
import jax.numpy as jnp
from jax import lax
from jax.experimental import pallas as pl
from jax.experimental.pallas import tpu as pltpu
from jax.sharding import PartitionSpec as P

BETA = 1.0
RIDGE = 0.1
AXES = ("gx", "gy", "gz")
ROWS_ROWS = (((1,), (1,)), ((), ()))
VMEM_BYTES = 36 * 2**20
PIVOTS = 8
UNROLL = 2
f32, bf16 = jnp.float32, jnp.bfloat16


def iota(shape, dim):
    return lax.broadcasted_iota(jnp.int32, shape, dim)


def half_rows(feats, classes):
    return -(-(feats * feats * classes // 128 + feats + 8) // 16) * 8


def moments_of(x, q, chunk=8):
    ny, feats, _ = x.shape
    scatter = first = None
    for c in range(0, ny, chunk):
        xs = jnp.concatenate([x[y] for y in range(c, c + chunk)], axis=1)
        qs = jnp.concatenate([q[y] for y in range(c, c + chunk)], axis=1)
        weighted = jnp.concatenate([xs[f : f + 1] * qs for f in range(feats)], axis=0)
        ones = jnp.ones((16, xs.shape[1]), bf16)
        s = lax.dot_general(xs, weighted, ROWS_ROWS, preferred_element_type=f32)
        m = lax.dot_general(
            jnp.concatenate([xs, ones], axis=0), qs, ROWS_ROWS, preferred_element_type=f32
        )
        scatter = s if scatter is None else scatter + s
        first = m if first is None else first + m
    return scatter, first


def no_moments(feats, classes):
    return jnp.zeros((feats, feats * classes), f32), jnp.zeros((feats + 16, classes), f32)


def put_moments(place_ref, mine, theirs, scatter, first):
    feats, lanes = scatter.shape
    rows = [scatter[:, j : j + 128] for j in range(0, lanes, 128)]
    rows.append(jnp.pad(first[: feats + 8], ((0, 0), (0, 128 - first.shape[1]))))
    half = mine.shape[0]
    rows.append(jnp.zeros((2 * half - sum(r.shape[0] for r in rows), 128), f32))
    rows = jnp.concatenate(rows, axis=0)
    odd = Place(place_ref, 1).sends == 1
    mine[...] = jnp.where(odd, rows[half:], rows[:half])
    theirs[pl.ds(0, half), :] = jnp.where(odd, rows[:half], rows[half:])


def all_moments(place_ref, mine, theirs):
    odd = Place(place_ref, 1).sends == 1
    mine, theirs = mine[...], theirs[...]
    return jnp.concatenate([jnp.where(odd, theirs, mine), jnp.where(odd, mine, theirs)], axis=0)


def m_step(total, w_ref, bias_ref):
    classes = bias_ref.shape[0]
    feats = w_ref.shape[0] // classes
    groups = 128 // classes
    tiles = feats // groups
    lane, sub = iota((8, 128), 1), iota((8, 128), 0)
    group = lane // classes

    def rows(r):
        return total[r : r + 8]

    def spread_lanes(v, g):
        return jnp.take_along_axis(v, lane % classes + g * classes, axis=1, mode="promise_in_bounds")

    def spread_row(v, r):
        return jnp.broadcast_to(v[r : r + 1], (8, 128))

    base = tiles * feats
    counts = spread_lanes(spread_row(rows(base + feats), 0), 0)
    inv = 1.0 / counts
    means = [spread_lanes(rows(base + 8 * j), 0) / counts for j in range(tiles)]
    eye = jnp.where(sub == group, 1.0, 0.0)
    zero = jnp.zeros((8, 128), f32)
    mean_row = [
        jnp.broadcast_to(jnp.sum(eye * m, axis=0, keepdims=True), (8, 128)) for m in means
    ]
    mat = [
        [rows(t * feats + 8 * j) * inv - means[j] * mean_row[t] + (RIDGE * eye if t == j else 0.0) for t in range(tiles)]
        for j in range(tiles)
    ]
    side = [[eye if t == j else zero for t in range(tiles)] for j in range(tiles)] + [mean_row]
    diag = [zero] * tiles
    for p in range(0, feats, PIVOTS):
        at, g0 = p // 8, p % 8
        cols = [("m", j) for j in range(at, tiles)] + [("s", j) for j in (*range(at + 1), tiles)]
        held = {"m": mat, "s": side}
        head = [{(n, j): spread_lanes(held[n][j][at], g0 + s) for n, j in cols} for s in range(PIVOTS)]
        e = [[spread_row(head[s]["m", at], g0 + t) for t in range(PIVOTS)] for s in range(PIVOTS)]
        factors = [
            [spread_row(mat[at][t], g0 + s) if t >= at else None for t in range(tiles)] for s in range(PIVOTS)
        ]
        ells, scaled = {}, []
        for s in range(PIVOTS):
            r = 1.0 / e[s][s]
            for t in range(s + 1, PIVOTS):
                ells[s, t] = e[s][t] * r
                for c in cols:
                    head[t][c] = head[t][c] - ells[s, t] * head[s][c]
                for u in range(t, PIVOTS):
                    e[t][u] = e[t][u] - ells[s, t] * e[s][u]
            scaled.append({c: head[s][c] * r for c in cols})
        for s in reversed(range(PIVOTS)):
            for t in range(s + 1, PIVOTS):
                for c in cols:
                    scaled[s][c] = scaled[s][c] - ells[s, t] * scaled[t][c]
        for t in range(at, tiles):
            for s in range(PIVOTS):
                factor = factors[s][t]
                if t == at:
                    factor = jnp.where(group >= g0 + PIVOTS, factor, 0.0)
                for n, j in cols:
                    held[n][j][t] = held[n][j][t] - factor * scaled[s][n, j]
        for s in range(PIVOTS):
            own = group == g0 + s
            for n, j in cols:
                if n == "s":
                    side[j][at] = jnp.where(own, head[s][n, j], side[j][at])
            diag[at] = jnp.where(own, e[s][s], diag[at])
    logdet = sum(jnp.log(d) for d in diag)
    step = classes
    while step < 128:
        logdet = logdet + pltpu.roll(logdet, step, 1)
        step *= 2
    everything = jnp.sum(counts, axis=1, keepdims=True) * (1.0 / groups)
    bias = jnp.log(counts / everything) - 0.5 * logdet
    for t in range(tiles):
        scale = lax.rsqrt(diag[t])
        shift = -side[tiles][t] * scale
        high = shift.astype(bf16).astype(f32)
        middle = (shift - high).astype(bf16).astype(f32)
        low = shift - high - middle
        parts = jnp.where(sub == 0, high, jnp.where(sub == 1, middle, jnp.where(sub == 2, low, 0.0)))
        block = [side[j][t] * scale for j in range(tiles)] + [parts, zero, bias]
        turned = jnp.concatenate(block + [zero] * (16 - len(block)), axis=0).T
        w_ref[pl.ds(t * 128, 128), :] = turned[:, : feats + 16].astype(bf16)
        if t == 0:
            bias_ref[...] = jnp.broadcast_to(turned[:classes, feats + 16 : feats + 17], (classes, 128))
    return means


def loglik_of(x, w_ref, bias):
    n, feats, nz = x.shape
    classes = bias.shape[0]
    xs = jnp.concatenate([x[j] for j in range(n)], axis=1)
    xs = jnp.concatenate([xs, jnp.ones((16, n * nz), bf16)], axis=0)
    white = jnp.dot(w_ref[...], xs, preferred_element_type=f32)
    white = white * white
    square = white[:classes]
    for g in range(1, feats):
        square = square + white[g * classes : (g + 1) * classes]
    return jnp.stack(
        [bias[:, :nz] - 0.5 * square[:, j * nz : (j + 1) * nz] for j in range(n)], axis=0
    )


def sharing(ny):
    return 128 // (2 * ny)


def own_lane(i, nx, ny, classes):
    start = 2 * ny * (i // (nx // sharing(ny)))
    lane, y = iota((ny, classes, 128), 2), iota((ny, classes, 128), 0)
    return (lane == start + y) | (lane == start + ny + y)


def shift_matrix(ny, nz):
    src, dst = iota((nz + 128, nz), 0), iota((nz + 128, nz), 1)
    near = (src < nz) & ((src == dst + 1) | (src == dst - 1))
    face = src - nz
    first = face % (2 * ny) < ny
    edge = (face >= 0) & ((first & (dst == nz - 1)) | (jnp.logical_not(first) & (dst == 0)))
    return jnp.where(near | edge, 1.0, 0.0).astype(bf16)


def take_matrix(ny, nz):
    src, dst = iota((nz, 128), 0), iota((nz, 128), 1)
    first = dst % (2 * ny) < ny
    hit = ((src == 0) & first) | ((src == nz - 1) & jnp.logical_not(first))
    return jnp.where(hit, 1.0, 0.0).astype(bf16)


def near_of(i, q_ref, y_halo, z_halo):
    nx, ny, classes, nz = q_ref.shape
    nx = nx - 2
    mid = q_ref[i + 1]
    down = q_ref[i].astype(f32)
    up = q_ref[i + 2].astype(f32)
    mid32 = mid.astype(f32)
    left = jnp.concatenate([y_halo[0, pl.ds(i, 1)], mid32[:-1]], axis=0)
    right = jnp.concatenate([mid32[1:], y_halo[1, pl.ds(i, 1)]], axis=0)
    face = z_halo[i % (nx // sharing(ny))]
    face = jnp.where(own_lane(i, nx, ny, classes), face[None], 0.0).astype(bf16)
    both = jnp.concatenate([mid, face], axis=2).reshape(ny * classes, nz + 128)
    along = jnp.dot(both, shift_matrix(ny, nz), preferred_element_type=f32)
    return (down + up) + (left + right) + along.reshape(ny, classes, nz)


def update_of(scores, near):
    s = scores + BETA * near
    e = jnp.exp(s - jnp.max(s, axis=1, keepdims=True))
    return (e * (1.0 / jnp.sum(e, axis=1, keepdims=True))).astype(bf16)


class Place:
    def __init__(self, place_ref, axis):
        self.sends, self.gets, self.before, self.after = (place_ref[4 * axis + j] for j in range(4))

    def halo(self, inner, outer):
        before = jnp.where(self.gets == 1, inner, outer)
        after = jnp.where(self.gets == 1, outer, inner)
        before = jnp.where(self.before == 1, before, 0.0)
        after = jnp.where(self.after == 1, after, 0.0)
        return before, after


def fill_halo(place_ref, halo, q_ref, padded, y_halo, z_halo):
    xi, xo, yi, yo, zi, zo = halo
    nx, ny, classes, nz = q_ref.shape
    before, after = Place(place_ref, 0).halo(xi[...].astype(f32), xo[...].astype(f32))
    padded[0], padded[nx + 1] = before.astype(bf16), after.astype(bf16)
    for i in range(nx):
        padded[i + 1] = q_ref[i]
    rows = y_halo.shape[1] * classes
    before, after = Place(place_ref, 1).halo(*(y[pl.ds(y.shape[0] - rows, rows), :] for y in (yi, yo)))
    y_halo[0], y_halo[1] = before.reshape(y_halo.shape[1:]), after.reshape(y_halo.shape[1:])
    rows = z_halo.shape[0] * classes
    before, after = Place(place_ref, 2).halo(*(z[pl.ds(z.shape[0] - rows, rows), :] for z in (zi, zo)))
    first = iota(before.shape, 1) % (2 * ny) < ny
    z_halo[...] = jnp.where(first, after, before).reshape(z_halo.shape)


def put_faces(place_ref, i, q, xin, xout, yin, yout, zface):
    ny, classes, nz = q.shape
    nx = yout.shape[0] // classes
    sends_x, sends_y = Place(place_ref, 0).sends, Place(place_ref, 1).sends

    @pl.when(((i == 0) & (sends_x == 1)) | ((i == nx - 1) & (sends_x == 0)))
    def _():
        xin[...] = q

    @pl.when(((i == 0) & (sends_x == 0)) | ((i == nx - 1) & (sends_x == 1)))
    def _():
        xout[...] = q

    first, last = q[0].astype(f32), q[ny - 1].astype(f32)
    yin[pl.ds(yin.shape[0] - yout.shape[0] + i * classes, classes), :] = jnp.where(sends_y == 1, first, last)
    yout[pl.ds(i * classes, classes), :] = jnp.where(sends_y == 1, last, first)
    spread = jnp.dot(q.reshape(ny * classes, nz), take_matrix(ny, nz), preferred_element_type=f32)
    spread = jnp.where(own_lane(i, nx, ny, classes), spread.reshape(ny, classes, 128), 0.0)
    spread = jnp.sum(spread, axis=0)
    share = nx // sharing(ny)
    at = pl.ds((i % share) * classes, classes)
    zface[at, :] = jnp.where(i < share, spread, zface[at, :] + spread)


def first_kernel(
    place, x_hbm, q_hbm, xt, qt, xin, xout, yout, zface, mine, theirs, x_in, q_in, sems
):
    nx, ny, feats, nz = xt.shape
    classes = qt.shape[2]

    def copies(i):
        return (
            pltpu.make_async_copy(q_hbm.at[:, i], q_in.at[i], sems.at[0, i]),
            pltpu.make_async_copy(x_hbm.at[:, i], x_in.at[i], sems.at[1, i]),
        )

    for i in range(nx):
        for copy in copies(i):
            copy.start()

    zface[...] = jnp.zeros_like(zface)

    def slab(i, sums):
        for copy in copies(i):
            copy.wait()
        x = jnp.swapaxes(x_in[i], 0, 1)
        q = jnp.swapaxes(q_in[i], 0, 1)
        xt[i] = x
        qt[i] = q
        put_faces(place, i, q, xin, xout, theirs, yout, zface)
        return jax.tree.map(jnp.add, sums, moments_of(x, q))

    sums = lax.fori_loop(0, nx, slab, no_moments(feats, classes), unroll=UNROLL)
    put_moments(place, mine, theirs, *sums)


def second_kernel(
    place, mine, theirs, xt, qt, xi, xo, yi, yo, zi, zo, sc, q1, xin, xout, yin, yout, zface, w, bias, *space
):
    nx, ny = xt.shape[:2]
    fill_halo(place, (xi, xo, yi, yo, zi, zo), qt, *space)
    m_step(all_moments(place, mine, theirs), w, bias)
    zface[...] = jnp.zeros_like(zface)

    def slab(i, carry):
        half = ny // 2
        sc[i, pl.ds(0, half)] = loglik_of(xt[i, pl.ds(0, half)], w, bias[...])
        sc[i, pl.ds(half, half)] = loglik_of(xt[i, pl.ds(half, half)], w, bias[...])
        q = update_of(sc[i], near_of(i, *space))
        q1[i] = q
        put_faces(place, i, q, xin, xout, yin, yout, zface)
        return carry

    lax.fori_loop(0, nx, slab, 0, unroll=UNROLL)


def third_kernel(place, sc, xt, qt, xi, xo, yi, yo, zi, zo, q2, xin, xout, yout, zface, mine, theirs, *space):
    nx, _, feats, _ = xt.shape
    classes = qt.shape[2]
    fill_halo(place, (xi, xo, yi, yo, zi, zo), qt, *space)
    zface[...] = jnp.zeros_like(zface)

    def slab(i, sums):
        q = update_of(sc[i], near_of(i, *space))
        q2[i] = q
        put_faces(place, i, q, xin, xout, theirs, yout, zface)
        return jax.tree.map(jnp.add, sums, moments_of(xt[i], q))

    sums = lax.fori_loop(0, nx, slab, no_moments(feats, classes), unroll=UNROLL)
    put_moments(place, mine, theirs, *sums)


def fourth_kernel(place, mine, theirs, xt, qt, xi, xo, yi, yo, zi, zo, seg, means_ref, w, bias, *space):
    nx, ny = xt.shape[:2]
    classes, feats = means_ref.shape
    fill_halo(place, (xi, xo, yi, yo, zi, zo), qt, *space)
    means = jnp.concatenate(m_step(all_moments(place, mine, theirs), w, bias), axis=0)
    means = jnp.concatenate([means, jnp.zeros((128 - feats, 128), f32)], axis=0).T
    means_ref[...] = means[:classes, :feats]

    def slab(i, carry):
        half = ny // 2
        scores = jnp.concatenate(
            [loglik_of(xt[i, pl.ds(j * half, half)], w, bias[...]) for j in range(2)], axis=0
        )
        q = update_of(scores, near_of(i, *space))
        seg[:, i] = jnp.swapaxes(q, 0, 1)
        return carry

    lax.fori_loop(0, nx, slab, 0, unroll=UNROLL)


def pairings(n):
    if n == 2:
        return [[1, 0]]
    if n == 4:
        return [[1, 0, 3, 2], [3, 2, 1, 0], [2, 3, 0, 1]]
    return None


def send(value, axis, to):
    return lax.ppermute(value, axis, list(enumerate(to)))


def place_along(axis):
    n, at = lax.axis_size(axis), lax.axis_index(axis)
    if pairings(n) is None:
        return [0 * at, 0 * at + 1, at > 0, at < n - 1]
    return [at % 2, at % 2, at > 0, at < n - 1]


def swap(axis, inner, outer):
    n = lax.axis_size(axis)
    if n == 2:
        got = send(inner, axis, [1, 0])
        return got, got
    if n == 4:
        return tuple(send(v, axis, to) for v, to in zip((inner, outer), pairings(n)))
    return send(inner, axis, [(i + 1) % n for i in range(n)]), send(outer, axis, [(i - 1) % n for i in range(n)])


def exchange(xin, xout, yin, yout, zface):
    return *swap("gx", xin, xout), *swap("gy", yin, yout), *swap("gz", zface, zface)


def sum_and_exchange(xin, xout, yout, zface, mine, theirs):
    rows = mine.shape[0]
    paired = lax.axis_size("gy") == 2
    if paired:
        yi = yo = send(theirs, "gy", [1, 0])
        total = mine + yi[:rows]
    else:
        yi, yo = swap("gy", theirs[rows:], yout)
        total = lax.psum(jnp.concatenate([mine, theirs[:rows]], axis=0), "gy")
    if lax.axis_size("gx") == 4:
        total = sum((send(total, "gx", to) for to in pairings(4)), total)
    else:
        total = lax.psum(total, "gx")
    total, xin, xout = lax.optimization_barrier((total, xin, xout))
    xi, xo = swap("gx", xin, xout)
    if lax.axis_size("gz") == 4:
        n = total.shape[0]
        both = jnp.concatenate([total, zface], axis=0)
        zi, zo = (send(both, "gz", to) for to in pairings(4)[:2])
        total = total + zi[:n] + zo[:n] + send(total, "gz", pairings(4)[2])
    else:
        zi, zo = swap("gz", zface, zface)
        total = lax.psum(total, "gz")
    total, xi, xo = lax.optimization_barrier((total, xi, xo))
    halves = (total, send(total, "gy", [1, 0])) if paired else (total[:rows], total[rows:])
    return *halves, xi, xo, yi, yo, zi, zo


def call(kernel, outs, scratch, places, *args, vmem=VMEM_BYTES):
    specs = [pl.BlockSpec(memory_space=place) for place in places]
    specs += [pl.BlockSpec(memory_space=pltpu.VMEM)] * (len(args) - len(places))
    return pl.pallas_call(
        kernel,
        out_shape=tuple(outs),
        in_specs=specs,
        out_specs=tuple(pl.BlockSpec(memory_space=pltpu.VMEM) for _ in outs),
        scratch_shapes=scratch,
        compiler_params=pltpu.CompilerParams(vmem_limit_bytes=vmem),
    )(*args)


def local(features, posteriors):
    feats, nx, ny, nz = features.shape
    classes = posteriors.shape[0]
    share = nx // sharing(ny)
    shape = jax.ShapeDtypeStruct
    brick = shape((nx, ny, classes, nz), bf16)
    face_x = shape((ny, classes, nz), bf16)
    face_y = shape((nx * classes, nz), f32)
    face_z = shape((share * classes, 128), f32)
    half = half_rows(feats, classes)
    mine, theirs = shape((half, 128), f32), shape((half + nx * classes, 128), f32)
    solved = [pltpu.VMEM((feats * classes, feats + 16), bf16), pltpu.VMEM((classes, 128), f32)]
    halos = [
        pltpu.VMEM((nx + 2, ny, classes, nz), bf16),
        pltpu.VMEM((2, nx, classes, nz), f32),
        pltpu.VMEM((share, classes, 128), f32),
    ]
    place = jnp.stack([jnp.asarray(v, jnp.int32) for axis in AXES for v in place_along(axis)])

    xt, qt, *edge = call(
        first_kernel,
        [shape((nx, ny, feats, nz), bf16), brick, face_x, face_x, face_y, face_z, mine, theirs],
        [
            pltpu.VMEM((nx, feats, ny, nz), bf16),
            pltpu.VMEM((nx, classes, ny, nz), bf16),
            pltpu.SemaphoreType.DMA((2, nx)),
        ],
        [pltpu.SMEM, pltpu.HBM, pltpu.HBM],
        place,
        features,
        posteriors,
        vmem=48 * 2**20,
    )
    *total, xi, xo, yi, yo, zi, zo = sum_and_exchange(*edge)
    halo = (xi, xo, yi, yo, zi, zo)
    sc, q1, *edge = call(
        second_kernel,
        [shape((nx, ny, classes, nz), f32), brick, face_x, face_x, face_y, face_y, face_z],
        solved + halos,
        [pltpu.SMEM],
        place,
        *total,
        xt,
        qt,
        *halo,
    )
    halo = exchange(*edge)
    q2, *edge = call(
        third_kernel,
        [brick, face_x, face_x, face_y, face_z, mine, theirs],
        halos,
        [pltpu.SMEM],
        place,
        sc,
        xt,
        q1,
        *halo,
    )
    *total, xi, xo, yi, yo, zi, zo = sum_and_exchange(*edge)
    halo = (xi, xo, yi, yo, zi, zo)
    return call(
        fourth_kernel,
        [shape(posteriors.shape, bf16), shape((classes, feats), f32)],
        solved + halos,
        [pltpu.SMEM],
        place,
        *total,
        xt,
        q2,
        *halo,
    )


def solution(mesh):
    placed = P(None, "gx", "gy", "gz")
    return jax.shard_map(
        local, mesh=mesh, in_specs=(placed, placed), out_specs=(placed, P()), check_vma=False
    )
```

```python
import jax
import jax.numpy as jnp
from jax import lax
from jax.experimental import pallas as pl
from jax.experimental.pallas import tpu as pltpu
from jax.sharding import PartitionSpec as P

BETA = 1.0
RIDGE = 0.1
AXES = ("gx", "gy", "gz")
ROWS_ROWS = (((1,), (1,)), ((), ()))
VMEM_BYTES = 36 * 2**20
PIVOTS = 8
VOXEL_ROWS = 8
CHUNK = 8
SPLIT = 2
f32, bf16 = jnp.float32, jnp.bfloat16


def iota(shape, dim):
    return lax.broadcasted_iota(jnp.int32, shape, dim)


def half_rows(feats, classes):
    return -(-(feats * feats * classes // 128 + feats + 8) // 16) * 8


def moments_of(x, q):
    ny, feats, _ = x.shape
    scatter = first = None
    chunk, part = CHUNK, feats // SPLIT
    for c in range(0, ny, chunk):
        xs = jnp.concatenate([x[y] for y in range(c, c + chunk)], axis=1)
        qs = jnp.concatenate([q[y] for y in range(c, c + chunk)], axis=1)
        ones = jnp.ones((16, xs.shape[1]), bf16)
        s = []
        for g in range(0, feats, part):
            weighted = jnp.concatenate([xs[f : f + 1] * qs for f in range(g, g + part)], axis=0)
            s.append(lax.dot_general(xs, weighted, ROWS_ROWS, preferred_element_type=f32))
        s = jnp.concatenate(s, axis=1)
        m = lax.dot_general(
            jnp.concatenate([xs, ones], axis=0), qs, ROWS_ROWS, preferred_element_type=f32
        )
        scatter = s if scatter is None else scatter + s
        first = m if first is None else first + m
    return scatter, first


def put_moments(place_ref, mine, theirs, scatter, first):
    feats, lanes = scatter.shape
    rows = [scatter[:, j : j + 128] for j in range(0, lanes, 128)]
    rows.append(jnp.pad(first[: feats + 8], ((0, 0), (0, 128 - first.shape[1]))))
    half = mine.shape[0]
    rows.append(jnp.zeros((2 * half - sum(r.shape[0] for r in rows), 128), f32))
    rows = jnp.concatenate(rows, axis=0)
    odd = Place(place_ref, 1).sends == 1
    mine[...] = jnp.where(odd, rows[half:], rows[:half])
    theirs[pl.ds(0, half), :] = jnp.where(odd, rows[:half], rows[half:])


def all_moments(place_ref, mine, theirs):
    odd = Place(place_ref, 1).sends == 1
    mine, theirs = mine[...], theirs[...]
    return jnp.concatenate([jnp.where(odd, theirs, mine), jnp.where(odd, mine, theirs)], axis=0)


def m_step(total, w_ref, bias_ref):
    classes = bias_ref.shape[0]
    feats = w_ref.shape[0] // classes
    groups = 128 // classes
    tiles = feats // groups
    lane, sub = iota((8, 128), 1), iota((8, 128), 0)
    group = lane // classes

    def rows(r):
        return total[r : r + 8]

    def spread_lanes(v, g):
        return jnp.take_along_axis(v, lane % classes + g * classes, axis=1, mode="promise_in_bounds")

    def spread_row(v, r):
        return jnp.broadcast_to(v[r : r + 1], (8, 128))

    base = tiles * feats
    counts = spread_lanes(spread_row(rows(base + feats), 0), 0)
    inv = 1.0 / counts
    means = [spread_lanes(rows(base + 8 * j), 0) / counts for j in range(tiles)]
    eye = jnp.where(sub == group, 1.0, 0.0)
    zero = jnp.zeros((8, 128), f32)
    mean_row = [
        jnp.broadcast_to(jnp.sum(eye * m, axis=0, keepdims=True), (8, 128)) for m in means
    ]
    mat = [
        [rows(t * feats + 8 * j) * inv - means[j] * mean_row[t] + (RIDGE * eye if t == j else 0.0) for t in range(tiles)]
        for j in range(tiles)
    ]
    side = [[eye if t == j else zero for t in range(tiles)] for j in range(tiles)] + [mean_row]
    diag = [zero] * tiles
    for p in range(0, feats, PIVOTS):
        at, g0 = p // 8, p % 8
        cols = [("m", j) for j in range(at, tiles)] + [("s", j) for j in (*range(at + 1), tiles)]
        held = {"m": mat, "s": side}
        head = [{(n, j): spread_lanes(held[n][j][at], g0 + s) for n, j in cols} for s in range(PIVOTS)]
        e = [[spread_row(head[s]["m", at], g0 + t) for t in range(PIVOTS)] for s in range(PIVOTS)]
        factors = [
            [spread_row(mat[at][t], g0 + s) if t >= at else None for t in range(tiles)] for s in range(PIVOTS)
        ]
        ells, scaled = {}, []
        for s in range(PIVOTS):
            r = 1.0 / e[s][s]
            for t in range(s + 1, PIVOTS):
                ells[s, t] = e[s][t] * r
                for c in cols:
                    head[t][c] = head[t][c] - ells[s, t] * head[s][c]
                for u in range(t, PIVOTS):
                    e[t][u] = e[t][u] - ells[s, t] * e[s][u]
            scaled.append({c: head[s][c] * r for c in cols})
        for s in reversed(range(PIVOTS)):
            for t in range(s + 1, PIVOTS):
                for c in cols:
                    scaled[s][c] = scaled[s][c] - ells[s, t] * scaled[t][c]
        for t in range(at, tiles):
            for s in range(PIVOTS):
                factor = factors[s][t]
                if t == at:
                    factor = jnp.where(group >= g0 + PIVOTS, factor, 0.0)
                for n, j in cols:
                    held[n][j][t] = held[n][j][t] - factor * scaled[s][n, j]
        for s in range(PIVOTS):
            own = group == g0 + s
            for n, j in cols:
                if n == "s":
                    side[j][at] = jnp.where(own, head[s][n, j], side[j][at])
            diag[at] = jnp.where(own, e[s][s], diag[at])
    logdet = sum(jnp.log(d) for d in diag)
    step = classes
    while step < 128:
        logdet = logdet + pltpu.roll(logdet, step, 1)
        step *= 2
    everything = jnp.sum(counts, axis=1, keepdims=True) * (1.0 / groups)
    bias = jnp.log(counts / everything) - 0.5 * logdet
    for t in range(tiles):
        scale = lax.rsqrt(diag[t])
        shift = -side[tiles][t] * scale
        high = shift.astype(bf16).astype(f32)
        middle = (shift - high).astype(bf16).astype(f32)
        low = shift - high - middle
        parts = jnp.where(sub == 0, high, jnp.where(sub == 1, middle, jnp.where(sub == 2, low, 0.0)))
        block = [side[j][t] * scale for j in range(tiles)] + [parts, zero, bias]
        turned = jnp.concatenate(block + [zero] * (16 - len(block)), axis=0).T
        w_ref[pl.ds(t * 128, 128), :] = turned[:, : feats + 16].astype(bf16)
        if t == 0:
            bias_ref[...] = jnp.broadcast_to(turned[:classes, feats + 16 : feats + 17], (classes, 128))
    return means


def loglik_of(x, w_ref, bias):
    parts = [loglik_part(x[j : j + VOXEL_ROWS], w_ref, bias) for j in range(0, x.shape[0], VOXEL_ROWS)]
    return jnp.concatenate(parts, axis=0)


def loglik_part(x, w_ref, bias):
    n, feats, nz = x.shape
    classes = bias.shape[0]
    xs = jnp.concatenate([x[j] for j in range(n)], axis=1)
    xs = jnp.concatenate([xs, jnp.ones((16, n * nz), bf16)], axis=0)
    white = jnp.dot(w_ref[...], xs, preferred_element_type=f32)
    white = white * white
    square = white[:classes]
    for g in range(1, feats):
        square = square + white[g * classes : (g + 1) * classes]
    return jnp.stack(
        [bias[:, :nz] - 0.5 * square[:, j * nz : (j + 1) * nz] for j in range(n)], axis=0
    )


def sharing(ny):
    return 128 // (2 * ny)


def own_lane(i, nx, ny, classes):
    start = 2 * ny * (i // (nx // sharing(ny)))
    lane, y = iota((ny, classes, 128), 2), iota((ny, classes, 128), 0)
    return (lane == start + y) | (lane == start + ny + y)


def shift_matrix(ny, nz):
    src, dst = iota((nz + 128, nz), 0), iota((nz + 128, nz), 1)
    near = (src < nz) & ((src == dst + 1) | (src == dst - 1))
    face = src - nz
    first = face % (2 * ny) < ny
    edge = (face >= 0) & ((first & (dst == nz - 1)) | (jnp.logical_not(first) & (dst == 0)))
    return jnp.where(near | edge, 1.0, 0.0).astype(bf16)


def take_matrix(ny, nz):
    src, dst = iota((nz, 128), 0), iota((nz, 128), 1)
    first = dst % (2 * ny) < ny
    hit = ((src == 0) & first) | ((src == nz - 1) & jnp.logical_not(first))
    return jnp.where(hit, 1.0, 0.0).astype(bf16)


def near_of(i, q_ref, y_halo, z_halo):
    nx, ny, classes, nz = q_ref.shape
    nx = nx - 2
    mid = q_ref[i + 1]
    down = q_ref[i].astype(f32)
    up = q_ref[i + 2].astype(f32)
    mid32 = mid.astype(f32)
    left = jnp.concatenate([y_halo[0, pl.ds(i, 1)], mid32[:-1]], axis=0)
    right = jnp.concatenate([mid32[1:], y_halo[1, pl.ds(i, 1)]], axis=0)
    face = z_halo[i % (nx // sharing(ny))]
    face = jnp.where(own_lane(i, nx, ny, classes), face[None], 0.0).astype(bf16)
    both = jnp.concatenate([mid, face], axis=2).reshape(ny * classes, nz + 128)
    along = jnp.dot(both, shift_matrix(ny, nz), preferred_element_type=f32)
    return (down + up) + (left + right) + along.reshape(ny, classes, nz)


def update_of(scores, near):
    s = scores + BETA * near
    e = jnp.exp(s - jnp.max(s, axis=1, keepdims=True))
    return (e * (1.0 / jnp.sum(e, axis=1, keepdims=True))).astype(bf16)


class Place:
    def __init__(self, place_ref, axis):
        self.sends, self.gets, self.before, self.after = (place_ref[4 * axis + j] for j in range(4))

    def halo(self, inner, outer):
        before = jnp.where(self.gets == 1, inner, outer)
        after = jnp.where(self.gets == 1, outer, inner)
        before = jnp.where(self.before == 1, before, 0.0)
        after = jnp.where(self.after == 1, after, 0.0)
        return before, after


def fill_halo(place_ref, halo, q_ref, padded, y_halo, z_halo):
    xi, xo, yi, yo, zi, zo = halo
    nx, ny, classes, nz = q_ref.shape
    before, after = Place(place_ref, 0).halo(xi[...].astype(f32), xo[...].astype(f32))
    padded[0], padded[nx + 1] = before.astype(bf16), after.astype(bf16)
    for i in range(nx):
        padded[i + 1] = q_ref[i]
    rows = y_halo.shape[1] * classes
    before, after = Place(place_ref, 1).halo(*(y[pl.ds(y.shape[0] - rows, rows), :] for y in (yi, yo)))
    y_halo[0], y_halo[1] = before.reshape(y_halo.shape[1:]), after.reshape(y_halo.shape[1:])
    rows = z_halo.shape[0] * classes
    before, after = Place(place_ref, 2).halo(*(z[pl.ds(z.shape[0] - rows, rows), :] for z in (zi, zo)))
    first = iota(before.shape, 1) % (2 * ny) < ny
    z_halo[...] = jnp.where(first, after, before).reshape(z_halo.shape)


def put_faces(place_ref, brick, xin, xout, yin, yout, zface):
    nx, ny, classes, nz = brick.shape
    first_in, first_in_y = Place(place_ref, 0).sends == 1, Place(place_ref, 1).sends == 1
    xin[...] = jnp.where(first_in, brick[0], brick[nx - 1])
    xout[...] = jnp.where(first_in, brick[nx - 1], brick[0])
    first = jnp.concatenate([brick[i, 0] for i in range(nx)], axis=0).astype(f32)
    last = jnp.concatenate([brick[i, ny - 1] for i in range(nx)], axis=0).astype(f32)
    rows = nx * classes
    yin[pl.ds(yin.shape[0] - rows, rows), :] = jnp.where(first_in_y, first, last)
    yout[...] = jnp.where(first_in_y, last, first)
    share = nx // sharing(ny)
    for j in range(share):
        total = None
        for i in range(j, nx, share):
            spread = jnp.dot(brick[i].reshape(ny * classes, nz), take_matrix(ny, nz), preferred_element_type=f32)
            spread = jnp.where(own_lane(i, nx, ny, classes), spread.reshape(ny, classes, 128), 0.0)
            spread = jnp.sum(spread, axis=0)
            total = spread if total is None else total + spread
        zface[pl.ds(j * classes, classes), :] = total


def first_kernel(place, x_hbm, q_hbm, xt, qt, xin, xout, yout, zface, mine, theirs, x_in, q_in, sems):
    nx = xt.shape[0]
    copies = [
        (
            pltpu.make_async_copy(q_hbm.at[:, i], q_in.at[i], sems.at[0, i]),
            pltpu.make_async_copy(x_hbm.at[:, i], x_in.at[i], sems.at[1, i]),
        )
        for i in range(nx)
    ]
    for pair in copies:
        for copy in pair:
            copy.start()
    sums = None
    for i in range(nx):
        for copy in copies[i]:
            copy.wait()
        xt[i] = jnp.swapaxes(x_in[i], 0, 1)
        qt[i] = jnp.swapaxes(q_in[i], 0, 1)
        here = moments_of(xt[i], qt[i])
        sums = here if sums is None else jax.tree.map(jnp.add, sums, here)
    put_faces(place, qt, xin, xout, theirs, yout, zface)
    put_moments(place, mine, theirs, *sums)


def second_kernel(
    place, mine, theirs, xt, qt, xi, xo, yi, yo, zi, zo, sc, q1, xin, xout, yin, yout, zface, w, bias, near, *space
):
    nx = xt.shape[0]
    fill_halo(place, (xi, xo, yi, yo, zi, zo), qt, *space)
    for i in range(nx):
        near[i] = near_of(i, *space)
    m_step(all_moments(place, mine, theirs), w, bias)
    for i in range(nx):
        scores = loglik_of(xt[i], w, bias[...])
        sc[i] = scores
        q1[i] = update_of(scores, near[i])
    put_faces(place, q1, xin, xout, yin, yout, zface)


def third_kernel(place, sc, xt, qt, xi, xo, yi, yo, zi, zo, q2, xin, xout, yout, zface, mine, theirs, *space):
    nx = xt.shape[0]
    fill_halo(place, (xi, xo, yi, yo, zi, zo), qt, *space)
    sums = None
    for i in range(nx):
        q = update_of(sc[i], near_of(i, *space))
        q2[i] = q
        here = moments_of(xt[i], q)
        sums = here if sums is None else jax.tree.map(jnp.add, sums, here)
    put_faces(place, q2, xin, xout, theirs, yout, zface)
    put_moments(place, mine, theirs, *sums)


def fourth_kernel(place, mine, theirs, xt, qt, xi, xo, yi, yo, zi, zo, seg, means_ref, w, bias, near, *space):
    nx = xt.shape[0]
    classes, feats = means_ref.shape
    fill_halo(place, (xi, xo, yi, yo, zi, zo), qt, *space)
    for i in range(nx):
        near[i] = near_of(i, *space)
    means = jnp.concatenate(m_step(all_moments(place, mine, theirs), w, bias), axis=0)
    means = jnp.concatenate([means, jnp.zeros((128 - feats, 128), f32)], axis=0).T
    means_ref[...] = means[:classes, :feats]
    for i in range(nx):
        q = update_of(loglik_of(xt[i], w, bias[...]), near[i])
        seg[:, i] = jnp.swapaxes(q, 0, 1)


def pairings(n):
    if n == 2:
        return [[1, 0]]
    if n == 4:
        return [[1, 0, 3, 2], [3, 2, 1, 0], [2, 3, 0, 1]]
    return None


def send(value, axis, to):
    return lax.ppermute(value, axis, list(enumerate(to)))


def place_along(axis):
    n, at = lax.axis_size(axis), lax.axis_index(axis)
    if pairings(n) is None:
        return [0 * at, 0 * at + 1, at > 0, at < n - 1]
    return [at % 2, at % 2, at > 0, at < n - 1]


def send_middle(value, axis, other):
    n = lax.axis_size(other)
    if n % 2:
        return send(value, axis, pairings(4)[1])
    pairs = []
    for a in range(4):
        for o in range(n):
            here, there = (a, o), (3 - a, o) if a in (1, 2) else (a, o ^ 1)
            if axis == "gx":
                pairs.append((here[0] * n + here[1], there[0] * n + there[1]))
            else:
                pairs.append((here[1] * 4 + here[0], there[1] * 4 + there[0]))
    return lax.ppermute(value, ("gx", "gz"), pairs)


def swap(axis, inner, outer):
    n = lax.axis_size(axis)
    if n == 2:
        got = send(inner, axis, [1, 0])
        return got, got
    if n == 4:
        return send(inner, axis, pairings(n)[0]), send_middle(outer, axis, "gz" if axis == "gx" else "gx")
    return send(inner, axis, [(i + 1) % n for i in range(n)]), send(outer, axis, [(i - 1) % n for i in range(n)])


def exchange(xin, xout, yin, yout, zface):
    return *swap("gx", xin, xout), *swap("gy", yin, yout), *swap("gz", zface, zface)


def sum_and_exchange(xin, xout, yout, zface, mine, theirs):
    rows = mine.shape[0]
    paired = lax.axis_size("gy") == 2
    if paired:
        yi = yo = send(theirs, "gy", [1, 0])
        total = mine + yi[:rows]
    else:
        yi, yo = swap("gy", theirs[rows:], yout)
        total = lax.psum(jnp.concatenate([mine, theirs[:rows]], axis=0), "gy")
    if lax.axis_size("gx") == 4:
        total = sum((send(total, "gx", to) for to in pairings(4)), total)
    else:
        total = lax.psum(total, "gx")
    total, xin, xout = lax.optimization_barrier((total, xin, xout))
    xi, xo = swap("gx", xin, xout)
    if lax.axis_size("gz") == 4:
        n = total.shape[0]
        both = jnp.concatenate([total, zface], axis=0)
        zi, zo = (send(both, "gz", to) for to in pairings(4)[:2])
        total = total + zi[:n] + zo[:n] + send(total, "gz", pairings(4)[2])
    else:
        zi, zo = swap("gz", zface, zface)
        total = lax.psum(total, "gz")
    halves = (total, send(total, "gy", [1, 0])) if paired else (total[:rows], total[rows:])
    return *halves, xi, xo, yi, yo, zi, zo


def call(kernel, outs, scratch, places, *args, vmem=VMEM_BYTES):
    specs = [pl.BlockSpec(memory_space=place) for place in places]
    specs += [pl.BlockSpec(memory_space=pltpu.VMEM)] * (len(args) - len(places))
    return pl.pallas_call(
        kernel,
        out_shape=tuple(outs),
        in_specs=specs,
        out_specs=tuple(pl.BlockSpec(memory_space=pltpu.VMEM) for _ in outs),
        scratch_shapes=scratch,
        compiler_params=pltpu.CompilerParams(vmem_limit_bytes=vmem),
    )(*args)


class Sizes:
    def __init__(self, feats, classes, nx, ny, nz):
        shape = jax.ShapeDtypeStruct
        half = half_rows(feats, classes)
        share = nx // sharing(ny)
        self.features = shape((nx, ny, feats, nz), bf16)
        self.scores = shape((nx, ny, classes, nz), f32)
        self.brick = shape((nx, ny, classes, nz), bf16)
        self.face_x = shape((ny, classes, nz), bf16)
        self.face_y = shape((nx * classes, nz), f32)
        self.face_z = shape((share * classes, 128), f32)
        self.mine = shape((half, 128), f32)
        self.theirs = shape((half + nx * classes, 128), f32)
        self.out = shape((classes, nx, ny, nz), bf16)
        self.means = shape((classes, feats), f32)
        self.solved = [
            pltpu.VMEM((feats * classes, feats + 16), bf16),
            pltpu.VMEM((classes, 128), f32),
            pltpu.VMEM((nx, ny, classes, nz), f32),
        ]
        self.halos = [
            pltpu.VMEM((nx + 2, ny, classes, nz), bf16),
            pltpu.VMEM((2, nx, classes, nz), f32),
            pltpu.VMEM((share, classes, 128), f32),
        ]
        self.arrived = [
            pltpu.VMEM((nx, feats, ny, nz), bf16),
            pltpu.VMEM((nx, classes, ny, nz), bf16),
            pltpu.SemaphoreType.DMA((2, nx)),
        ]


def run_first(z, place, features, posteriors):
    outs = [z.features, z.brick, z.face_x, z.face_x, z.face_y, z.face_z, z.mine, z.theirs]
    places = [pltpu.SMEM, pltpu.HBM, pltpu.HBM]
    return call(first_kernel, outs, z.arrived, places, place, features, posteriors, vmem=48 * 2**20)


def run_second(z, place, mine, theirs, xt, qt, *halo):
    outs = [z.scores, z.brick, z.face_x, z.face_x, z.face_y, z.face_y, z.face_z]
    return call(second_kernel, outs, z.solved + z.halos, [pltpu.SMEM], place, mine, theirs, xt, qt, *halo)


def run_third(z, place, sc, xt, qt, *halo):
    outs = [z.brick, z.face_x, z.face_x, z.face_y, z.face_z, z.mine, z.theirs]
    return call(third_kernel, outs, z.halos, [pltpu.SMEM], place, sc, xt, qt, *halo)


def run_fourth(z, place, mine, theirs, xt, qt, *halo):
    return call(
        fourth_kernel, [z.out, z.means], z.solved + z.halos, [pltpu.SMEM], place, mine, theirs, xt, qt, *halo
    )


def local(features, posteriors):
    feats, nx, ny, nz = features.shape
    z = Sizes(feats, posteriors.shape[0], nx, ny, nz)
    place = jnp.stack([jnp.asarray(v, jnp.int32) for axis in AXES for v in place_along(axis)])
    xt, qt, *edge = run_first(z, place, features, posteriors)
    mine, theirs, *halo = sum_and_exchange(*edge)
    sc, q1, *edge = run_second(z, place, mine, theirs, xt, qt, *halo)
    halo = exchange(*edge)
    q2, *edge = run_third(z, place, sc, xt, q1, *halo)
    mine, theirs, *halo = sum_and_exchange(*edge)
    return run_fourth(z, place, mine, theirs, xt, q2, *halo)


def solution(mesh):
    placed = P(None, "gx", "gy", "gz")
    return jax.shard_map(
        local, mesh=mesh, in_specs=(placed, placed), out_specs=(placed, P()), check_vma=False
    )
```

```python
import jax
import jax.numpy as jnp
from jax import lax
from jax.experimental import pallas as pl
from jax.experimental.pallas import tpu as pltpu
from jax.sharding import PartitionSpec as P

BETA = 1.0
RIDGE = 0.1
AXES = ("gx", "gy", "gz")
ROWS_ROWS = (((1,), (1,)), ((), ()))
VMEM_BYTES = 36 * 2**20
PIVOTS = 8
VOXEL_ROWS = 8
CHUNK = 8
SPLIT = 2
TOGETHER = {"first": 4, "near": 8, "second": 4, "third": 8, "fourth": 4}
f32, bf16 = jnp.float32, jnp.bfloat16


def iota(shape, dim):
    return lax.broadcasted_iota(jnp.int32, shape, dim)


def half_rows(feats, classes):
    return -(-(feats * feats * classes // 128 + feats + 8) // 16) * 8


def moments_of(x, q):
    ny, feats, _ = x.shape
    scatter = first = None
    chunk, part = CHUNK, feats // SPLIT
    for c in range(0, ny, chunk):
        xs = jnp.concatenate([x[y] for y in range(c, c + chunk)], axis=1)
        qs = jnp.concatenate([q[y] for y in range(c, c + chunk)], axis=1)
        ones = jnp.ones((16, xs.shape[1]), bf16)
        s = []
        for g in range(0, feats, part):
            weighted = jnp.concatenate([xs[f : f + 1] * qs for f in range(g, g + part)], axis=0)
            s.append(lax.dot_general(xs, weighted, ROWS_ROWS, preferred_element_type=f32))
        s = jnp.concatenate(s, axis=1)
        m = lax.dot_general(
            jnp.concatenate([xs, ones], axis=0), qs, ROWS_ROWS, preferred_element_type=f32
        )
        scatter = s if scatter is None else scatter + s
        first = m if first is None else first + m
    return scatter, first


def no_moments(feats, classes):
    return jnp.zeros((feats, feats * classes), f32), jnp.zeros((feats + 16, classes), f32)


def put_moments(place_ref, mine, theirs, scatter, first):
    feats, lanes = scatter.shape
    rows = [scatter[:, j : j + 128] for j in range(0, lanes, 128)]
    rows.append(jnp.pad(first[: feats + 8], ((0, 0), (0, 128 - first.shape[1]))))
    half = mine.shape[0]
    rows.append(jnp.zeros((2 * half - sum(r.shape[0] for r in rows), 128), f32))
    rows = jnp.concatenate(rows, axis=0)
    odd = Place(place_ref, 1).sends == 1
    mine[...] = jnp.where(odd, rows[half:], rows[:half])
    theirs[pl.ds(0, half), :] = jnp.where(odd, rows[:half], rows[half:])


def all_moments(place_ref, mine, theirs):
    odd = Place(place_ref, 1).sends == 1
    mine, theirs = mine[...], theirs[...]
    return jnp.concatenate([jnp.where(odd, theirs, mine), jnp.where(odd, mine, theirs)], axis=0)


def m_step(total, w_ref, bias_ref):
    classes = bias_ref.shape[0]
    feats = w_ref.shape[0] // classes
    groups = 128 // classes
    tiles = feats // groups
    lane, sub = iota((8, 128), 1), iota((8, 128), 0)
    group = lane // classes

    def rows(r):
        return total[r : r + 8]

    def spread_lanes(v, g):
        return jnp.take_along_axis(v, lane % classes + g * classes, axis=1, mode="promise_in_bounds")

    def spread_row(v, r):
        return jnp.broadcast_to(v[r : r + 1], (8, 128))

    base = tiles * feats
    counts = spread_lanes(spread_row(rows(base + feats), 0), 0)
    inv = 1.0 / counts
    means = [spread_lanes(rows(base + 8 * j), 0) / counts for j in range(tiles)]
    eye = jnp.where(sub == group, 1.0, 0.0)
    zero = jnp.zeros((8, 128), f32)
    mean_row = [
        jnp.broadcast_to(jnp.sum(eye * m, axis=0, keepdims=True), (8, 128)) for m in means
    ]
    mat = [
        [rows(t * feats + 8 * j) * inv - means[j] * mean_row[t] + (RIDGE * eye if t == j else 0.0) for t in range(tiles)]
        for j in range(tiles)
    ]
    side = [[eye if t == j else zero for t in range(tiles)] for j in range(tiles)] + [mean_row]
    diag = [zero] * tiles
    for p in range(0, feats, PIVOTS):
        at, g0 = p // 8, p % 8
        cols = [("m", j) for j in range(at, tiles)] + [("s", j) for j in (*range(at + 1), tiles)]
        held = {"m": mat, "s": side}
        head = [{(n, j): spread_lanes(held[n][j][at], g0 + s) for n, j in cols} for s in range(PIVOTS)]
        e = [[spread_row(head[s]["m", at], g0 + t) for t in range(PIVOTS)] for s in range(PIVOTS)]
        factors = [
            [spread_row(mat[at][t], g0 + s) if t >= at else None for t in range(tiles)] for s in range(PIVOTS)
        ]
        ells, scaled = {}, []
        for s in range(PIVOTS):
            r = 1.0 / e[s][s]
            for t in range(s + 1, PIVOTS):
                ells[s, t] = e[s][t] * r
                for c in cols:
                    head[t][c] = head[t][c] - ells[s, t] * head[s][c]
                for u in range(t, PIVOTS):
                    e[t][u] = e[t][u] - ells[s, t] * e[s][u]
            scaled.append({c: head[s][c] * r for c in cols})
        for s in reversed(range(PIVOTS)):
            for t in range(s + 1, PIVOTS):
                for c in cols:
                    scaled[s][c] = scaled[s][c] - ells[s, t] * scaled[t][c]
        for t in range(at, tiles):
            for s in range(PIVOTS):
                factor = factors[s][t]
                if t == at:
                    factor = jnp.where(group >= g0 + PIVOTS, factor, 0.0)
                for n, j in cols:
                    held[n][j][t] = held[n][j][t] - factor * scaled[s][n, j]
        for s in range(PIVOTS):
            own = group == g0 + s
            for n, j in cols:
                if n == "s":
                    side[j][at] = jnp.where(own, head[s][n, j], side[j][at])
            diag[at] = jnp.where(own, e[s][s], diag[at])
    logdet = sum(jnp.log(d) for d in diag)
    step = classes
    while step < 128:
        logdet = logdet + pltpu.roll(logdet, step, 1)
        step *= 2
    everything = jnp.sum(counts, axis=1, keepdims=True) * (1.0 / groups)
    bias = jnp.log(counts / everything) - 0.5 * logdet
    for t in range(tiles):
        scale = lax.rsqrt(diag[t])
        shift = -side[tiles][t] * scale
        high = shift.astype(bf16).astype(f32)
        middle = (shift - high).astype(bf16).astype(f32)
        low = shift - high - middle
        parts = jnp.where(sub == 0, high, jnp.where(sub == 1, middle, jnp.where(sub == 2, low, 0.0)))
        block = [side[j][t] * scale for j in range(tiles)] + [parts, zero, bias]
        turned = jnp.concatenate(block + [zero] * (16 - len(block)), axis=0).T
        w_ref[pl.ds(t * 128, 128), :] = turned[:, : feats + 16].astype(bf16)
        if t == 0:
            bias_ref[...] = jnp.broadcast_to(turned[:classes, feats + 16 : feats + 17], (classes, 128))
    return means


def loglik_of(x, w_ref, bias):
    parts = [loglik_part(x[j : j + VOXEL_ROWS], w_ref, bias) for j in range(0, x.shape[0], VOXEL_ROWS)]
    return jnp.concatenate(parts, axis=0)


def loglik_part(x, w_ref, bias):
    n, feats, nz = x.shape
    classes = bias.shape[0]
    xs = jnp.concatenate([x[j] for j in range(n)], axis=1)
    xs = jnp.concatenate([xs, jnp.ones((16, n * nz), bf16)], axis=0)
    white = jnp.dot(w_ref[...], xs, preferred_element_type=f32)
    white = white * white
    square = white[:classes]
    for g in range(1, feats):
        square = square + white[g * classes : (g + 1) * classes]
    return jnp.stack(
        [bias[:, :nz] - 0.5 * square[:, j * nz : (j + 1) * nz] for j in range(n)], axis=0
    )


def sharing(ny):
    return 128 // (2 * ny)


def own_lane(i, nx, ny, classes):
    start = 2 * ny * (i // (nx // sharing(ny)))
    lane, y = iota((ny, classes, 128), 2), iota((ny, classes, 128), 0)
    return (lane == start + y) | (lane == start + ny + y)


def shift_matrix(ny, nz):
    src, dst = iota((nz + 128, nz), 0), iota((nz + 128, nz), 1)
    near = (src < nz) & ((src == dst + 1) | (src == dst - 1))
    face = src - nz
    first = face % (2 * ny) < ny
    edge = (face >= 0) & ((first & (dst == nz - 1)) | (jnp.logical_not(first) & (dst == 0)))
    return jnp.where(near | edge, 1.0, 0.0).astype(bf16)


def take_matrix(ny, nz):
    src, dst = iota((nz, 128), 0), iota((nz, 128), 1)
    first = dst % (2 * ny) < ny
    hit = ((src == 0) & first) | ((src == nz - 1) & jnp.logical_not(first))
    return jnp.where(hit, 1.0, 0.0).astype(bf16)


def near_of(i, q_ref, y_halo, z_halo):
    nx, ny, classes, nz = q_ref.shape
    nx = nx - 2
    mid = q_ref[i + 1]
    down = q_ref[i].astype(f32)
    up = q_ref[i + 2].astype(f32)
    mid32 = mid.astype(f32)
    left = jnp.concatenate([y_halo[0, pl.ds(i, 1)], mid32[:-1]], axis=0)
    right = jnp.concatenate([mid32[1:], y_halo[1, pl.ds(i, 1)]], axis=0)
    face = z_halo[i % (nx // sharing(ny))]
    face = jnp.where(own_lane(i, nx, ny, classes), face[None], 0.0).astype(bf16)
    both = jnp.concatenate([mid, face], axis=2).reshape(ny * classes, nz + 128)
    along = jnp.dot(both, shift_matrix(ny, nz), preferred_element_type=f32)
    return (down + up) + (left + right) + along.reshape(ny, classes, nz)


def update_of(scores, near):
    s = scores + BETA * near
    e = jnp.exp(s - jnp.max(s, axis=1, keepdims=True))
    return (e * (1.0 / jnp.sum(e, axis=1, keepdims=True))).astype(bf16)


class Place:
    def __init__(self, place_ref, axis):
        self.sends, self.gets, self.before, self.after = (place_ref[4 * axis + j] for j in range(4))

    def halo(self, inner, outer):
        before = jnp.where(self.gets == 1, inner, outer)
        after = jnp.where(self.gets == 1, outer, inner)
        before = jnp.where(self.before == 1, before, 0.0)
        after = jnp.where(self.after == 1, after, 0.0)
        return before, after


def fill_halo(place_ref, halo, q_ref, padded, y_halo, z_halo):
    xi, xo, yi, yo, zi, zo = halo
    nx, ny, classes, nz = q_ref.shape
    before, after = Place(place_ref, 0).halo(xi[...].astype(f32), xo[...].astype(f32))
    padded[0], padded[nx + 1] = before.astype(bf16), after.astype(bf16)
    for i in range(nx):
        padded[i + 1] = q_ref[i]
    rows = y_halo.shape[1] * classes
    before, after = Place(place_ref, 1).halo(*(y[pl.ds(y.shape[0] - rows, rows), :] for y in (yi, yo)))
    y_halo[0], y_halo[1] = before.reshape(y_halo.shape[1:]), after.reshape(y_halo.shape[1:])
    rows = z_halo.shape[0] * classes
    before, after = Place(place_ref, 2).halo(*(z[pl.ds(z.shape[0] - rows, rows), :] for z in (zi, zo)))
    first = iota(before.shape, 1) % (2 * ny) < ny
    z_halo[...] = jnp.where(first, after, before).reshape(z_halo.shape)


def put_faces(place_ref, brick, xin, xout, yin, yout, zface):
    nx, ny, classes, nz = brick.shape
    first_in, first_in_y = Place(place_ref, 0).sends == 1, Place(place_ref, 1).sends == 1
    xin[...] = jnp.where(first_in, brick[0], brick[nx - 1])
    xout[...] = jnp.where(first_in, brick[nx - 1], brick[0])
    first = jnp.concatenate([brick[i, 0] for i in range(nx)], axis=0).astype(f32)
    last = jnp.concatenate([brick[i, ny - 1] for i in range(nx)], axis=0).astype(f32)
    rows = nx * classes
    yin[pl.ds(yin.shape[0] - rows, rows), :] = jnp.where(first_in_y, first, last)
    yout[...] = jnp.where(first_in_y, last, first)
    share = nx // sharing(ny)
    for j in range(share):
        total = None
        for i in range(j, nx, share):
            spread = jnp.dot(brick[i].reshape(ny * classes, nz), take_matrix(ny, nz), preferred_element_type=f32)
            spread = jnp.where(own_lane(i, nx, ny, classes), spread.reshape(ny, classes, 128), 0.0)
            spread = jnp.sum(spread, axis=0)
            total = spread if total is None else total + spread
        zface[pl.ds(j * classes, classes), :] = total


def over_slabs(nx, together, body, carry=None):
    def step(j, carry):
        for i in range(together):
            carry = body(j * together + i, carry)
        return carry

    if together == nx:
        return step(0, carry)
    return lax.fori_loop(0, nx // together, step, carry)


def all_near(near, space):
    def body(i, carry):
        near[i] = near_of(i, *space)
        return carry

    over_slabs(near.shape[0], TOGETHER["near"], body, 0)


def first_kernel(place, x_hbm, q_hbm, xt, qt, xin, xout, yout, zface, mine, theirs, x_in, q_in, sems):
    nx = xt.shape[0]
    feats, classes = xt.shape[2], qt.shape[2]

    def copies(i):
        return (
            pltpu.make_async_copy(q_hbm.at[:, i], q_in.at[i], sems.at[0, i]),
            pltpu.make_async_copy(x_hbm.at[:, i], x_in.at[i], sems.at[1, i]),
        )

    for i in range(nx):
        for copy in copies(i):
            copy.start()

    def slab(i, sums):
        for copy in copies(i):
            copy.wait()
        x = jnp.swapaxes(x_in[i], 0, 1)
        q = jnp.swapaxes(q_in[i], 0, 1)
        xt[i], qt[i] = x, q
        return jax.tree.map(jnp.add, sums, moments_of(x, q))

    sums = over_slabs(nx, TOGETHER["first"], slab, no_moments(feats, classes))
    put_faces(place, qt, xin, xout, theirs, yout, zface)
    put_moments(place, mine, theirs, *sums)


def second_kernel(
    place, mine, theirs, xt, qt, xi, xo, yi, yo, zi, zo, sc, q1, xin, xout, yin, yout, zface, w, bias, near, *space
):
    nx = xt.shape[0]
    fill_halo(place, (xi, xo, yi, yo, zi, zo), qt, *space)
    all_near(near, space)
    m_step(all_moments(place, mine, theirs), w, bias)

    def slab(i, carry):
        scores = loglik_of(xt[i], w, bias[...])
        sc[i] = scores
        q1[i] = update_of(scores, near[i])
        return carry

    over_slabs(nx, TOGETHER["second"], slab, 0)
    put_faces(place, q1, xin, xout, yin, yout, zface)


def third_kernel(place, sc, xt, qt, xi, xo, yi, yo, zi, zo, q2, xin, xout, yout, zface, mine, theirs, *space):
    nx = xt.shape[0]
    fill_halo(place, (xi, xo, yi, yo, zi, zo), qt, *space)

    def slab(i, sums):
        q = update_of(sc[i], near_of(i, *space))
        q2[i] = q
        return jax.tree.map(jnp.add, sums, moments_of(xt[i], q))

    sums = over_slabs(nx, TOGETHER["third"], slab, no_moments(xt.shape[2], qt.shape[2]))
    put_faces(place, q2, xin, xout, theirs, yout, zface)
    put_moments(place, mine, theirs, *sums)


def fourth_kernel(place, mine, theirs, xt, qt, xi, xo, yi, yo, zi, zo, seg, means_ref, w, bias, near, *space):
    nx = xt.shape[0]
    classes, feats = means_ref.shape
    fill_halo(place, (xi, xo, yi, yo, zi, zo), qt, *space)
    all_near(near, space)
    means = jnp.concatenate(m_step(all_moments(place, mine, theirs), w, bias), axis=0)
    means = jnp.concatenate([means, jnp.zeros((128 - feats, 128), f32)], axis=0).T
    means_ref[...] = means[:classes, :feats]

    def slab(i, carry):
        q = update_of(loglik_of(xt[i], w, bias[...]), near[i])
        seg[:, i] = jnp.swapaxes(q, 0, 1)
        return carry

    over_slabs(nx, TOGETHER["fourth"], slab, 0)


def pairings(n):
    if n == 2:
        return [[1, 0]]
    if n == 4:
        return [[1, 0, 3, 2], [3, 2, 1, 0], [2, 3, 0, 1]]
    return None


def send(value, axis, to):
    return lax.ppermute(value, axis, list(enumerate(to)))


def place_along(axis):
    n, at = lax.axis_size(axis), lax.axis_index(axis)
    if pairings(n) is None:
        return [0 * at, 0 * at + 1, at > 0, at < n - 1]
    return [at % 2, at % 2, at > 0, at < n - 1]


def send_middle(value, axis, other):
    n = lax.axis_size(other)
    if n % 2:
        return send(value, axis, pairings(4)[1])
    pairs = []
    for a in range(4):
        for o in range(n):
            here, there = (a, o), (3 - a, o) if a in (1, 2) else (a, o ^ 1)
            if axis == "gx":
                pairs.append((here[0] * n + here[1], there[0] * n + there[1]))
            else:
                pairs.append((here[1] * 4 + here[0], there[1] * 4 + there[0]))
    return lax.ppermute(value, ("gx", "gz"), pairs)


def swap(axis, inner, outer):
    n = lax.axis_size(axis)
    if n == 2:
        got = send(inner, axis, [1, 0])
        return got, got
    if n == 4:
        return send(inner, axis, pairings(n)[0]), send_middle(outer, axis, "gz" if axis == "gx" else "gx")
    return send(inner, axis, [(i + 1) % n for i in range(n)]), send(outer, axis, [(i - 1) % n for i in range(n)])


def exchange(xin, xout, yin, yout, zface):
    return *swap("gx", xin, xout), *swap("gy", yin, yout), *swap("gz", zface, zface)


def sum_and_exchange(xin, xout, yout, zface, mine, theirs):
    rows = mine.shape[0]
    paired = lax.axis_size("gy") == 2
    if paired:
        yi = yo = send(theirs, "gy", [1, 0])
        total = mine + yi[:rows]
    else:
        yi, yo = swap("gy", theirs[rows:], yout)
        total = lax.psum(jnp.concatenate([mine, theirs[:rows]], axis=0), "gy")
    if lax.axis_size("gx") == 4:
        total = sum((send(total, "gx", to) for to in pairings(4)), total)
    else:
        total = lax.psum(total, "gx")
    total, xin, xout = lax.optimization_barrier((total, xin, xout))
    xi, xo = swap("gx", xin, xout)
    if lax.axis_size("gz") == 4:
        n = total.shape[0]
        both = jnp.concatenate([total, zface], axis=0)
        zi, zo = (send(both, "gz", to) for to in pairings(4)[:2])
        total = total + zi[:n] + zo[:n] + send(total, "gz", pairings(4)[2])
    else:
        zi, zo = swap("gz", zface, zface)
        total = lax.psum(total, "gz")
    halves = (total, send(total, "gy", [1, 0])) if paired else (total[:rows], total[rows:])
    return *halves, xi, xo, yi, yo, zi, zo


def call(kernel, outs, scratch, places, *args, vmem=VMEM_BYTES):
    specs = [pl.BlockSpec(memory_space=place) for place in places]
    specs += [pl.BlockSpec(memory_space=pltpu.VMEM)] * (len(args) - len(places))
    return pl.pallas_call(
        kernel,
        out_shape=tuple(outs),
        in_specs=specs,
        out_specs=tuple(pl.BlockSpec(memory_space=pltpu.VMEM) for _ in outs),
        scratch_shapes=scratch,
        compiler_params=pltpu.CompilerParams(vmem_limit_bytes=vmem),
    )(*args)


class Sizes:
    def __init__(self, feats, classes, nx, ny, nz):
        shape = jax.ShapeDtypeStruct
        half = half_rows(feats, classes)
        share = nx // sharing(ny)
        self.features = shape((nx, ny, feats, nz), bf16)
        self.scores = shape((nx, ny, classes, nz), f32)
        self.brick = shape((nx, ny, classes, nz), bf16)
        self.face_x = shape((ny, classes, nz), bf16)
        self.face_y = shape((nx * classes, nz), f32)
        self.face_z = shape((share * classes, 128), f32)
        self.mine = shape((half, 128), f32)
        self.theirs = shape((half + nx * classes, 128), f32)
        self.out = shape((classes, nx, ny, nz), bf16)
        self.means = shape((classes, feats), f32)
        self.solved = [
            pltpu.VMEM((feats * classes, feats + 16), bf16),
            pltpu.VMEM((classes, 128), f32),
            pltpu.VMEM((nx, ny, classes, nz), f32),
        ]
        self.halos = [
            pltpu.VMEM((nx + 2, ny, classes, nz), bf16),
            pltpu.VMEM((2, nx, classes, nz), f32),
            pltpu.VMEM((share, classes, 128), f32),
        ]
        self.arrived = [
            pltpu.VMEM((nx, feats, ny, nz), bf16),
            pltpu.VMEM((nx, classes, ny, nz), bf16),
            pltpu.SemaphoreType.DMA((2, nx)),
        ]


def run_first(z, place, features, posteriors):
    outs = [z.features, z.brick, z.face_x, z.face_x, z.face_y, z.face_z, z.mine, z.theirs]
    places = [pltpu.SMEM, pltpu.HBM, pltpu.HBM]
    return call(first_kernel, outs, z.arrived, places, place, features, posteriors, vmem=48 * 2**20)


def run_second(z, place, mine, theirs, xt, qt, *halo):
    outs = [z.scores, z.brick, z.face_x, z.face_x, z.face_y, z.face_y, z.face_z]
    return call(second_kernel, outs, z.solved + z.halos, [pltpu.SMEM], place, mine, theirs, xt, qt, *halo)


def run_third(z, place, sc, xt, qt, *halo):
    outs = [z.brick, z.face_x, z.face_x, z.face_y, z.face_z, z.mine, z.theirs]
    return call(third_kernel, outs, z.halos, [pltpu.SMEM], place, sc, xt, qt, *halo)


def run_fourth(z, place, mine, theirs, xt, qt, *halo):
    return call(
        fourth_kernel, [z.out, z.means], z.solved + z.halos, [pltpu.SMEM], place, mine, theirs, xt, qt, *halo
    )


def local(features, posteriors):
    feats, nx, ny, nz = features.shape
    z = Sizes(feats, posteriors.shape[0], nx, ny, nz)
    place = jnp.stack([jnp.asarray(v, jnp.int32) for axis in AXES for v in place_along(axis)])
    xt, qt, *edge = run_first(z, place, features, posteriors)
    mine, theirs, *halo = sum_and_exchange(*edge)
    sc, q1, *edge = run_second(z, place, mine, theirs, xt, qt, *halo)
    halo = exchange(*edge)
    q2, *edge = run_third(z, place, sc, xt, q1, *halo)
    mine, theirs, *halo = sum_and_exchange(*edge)
    return run_fourth(z, place, mine, theirs, xt, q2, *halo)


def solution(mesh):
    placed = P(None, "gx", "gy", "gz")
    return jax.shard_map(
        local, mesh=mesh, in_specs=(placed, placed), out_specs=(placed, P()), check_vma=False
    )
```

```python
import jax
import jax.numpy as jnp
from jax import lax
from jax.experimental import pallas as pl
from jax.experimental.pallas import tpu as pltpu
from jax.sharding import PartitionSpec as P

BETA = 1.0
RIDGE = 0.1
AXES = ("gx", "gy", "gz")
ROWS_ROWS = (((1,), (1,)), ((), ()))
VMEM_BYTES = 36 * 2**20
PIVOTS = 8
VOXEL_ROWS = 8
CHUNK = 8
TOGETHER = {"first": 4, "near": 8, "second": 4, "third": 8, "fourth": 4}
f32, bf16 = jnp.float32, jnp.bfloat16


def iota(shape, dim):
    return lax.broadcasted_iota(jnp.int32, shape, dim)


def half_rows(feats, classes):
    return -(-(feats * feats * classes // 128 + feats + 8) // 16) * 8


def moments_of(x, q):
    ny, feats, _ = x.shape
    last = feats - 128 // q.shape[1]
    sums = None
    for c in range(0, ny, CHUNK):
        xs = jnp.concatenate([x[y] for y in range(c, c + CHUNK)], axis=1)
        qs = jnp.concatenate([q[y] for y in range(c, c + CHUNK)], axis=1)
        ones = jnp.ones((16, xs.shape[1]), bf16)
        weighted = [xs[f : f + 1] * qs for f in range(feats)]
        here = (
            lax.dot_general(xs, jnp.concatenate(weighted[:last], axis=0), ROWS_ROWS, preferred_element_type=f32),
            lax.dot_general(
                jnp.concatenate([*weighted[last:], qs], axis=0),
                jnp.concatenate([xs, ones], axis=0),
                ROWS_ROWS,
                preferred_element_type=f32,
            ),
        )
        sums = here if sums is None else jax.tree.map(jnp.add, sums, here)
    return sums


def no_moments(feats, classes):
    return jnp.zeros((feats, feats * classes - 128), f32), jnp.zeros((128 + classes, feats + 16), f32)


def put_moments(place_ref, mine, theirs, scatter, rest):
    feats, lanes = scatter.shape
    rows = [scatter[:, j : j + 128] for j in range(0, lanes, 128)]
    rest = jnp.pad(rest, ((0, 256 - rest.shape[0]), (0, 128 - rest.shape[1])))
    rows.append(rest[:128].T[:feats])
    rows.append(rest[128:].T[: feats + 8])
    half = mine.shape[0]
    rows.append(jnp.zeros((2 * half - sum(r.shape[0] for r in rows), 128), f32))
    rows = jnp.concatenate(rows, axis=0)
    odd = Place(place_ref, 1).sends == 1
    mine[...] = jnp.where(odd, rows[half:], rows[:half])
    theirs[pl.ds(0, half), :] = jnp.where(odd, rows[:half], rows[half:])


def all_moments(place_ref, mine, theirs):
    odd = Place(place_ref, 1).sends == 1
    mine, theirs = mine[...], theirs[...]
    return jnp.concatenate([jnp.where(odd, theirs, mine), jnp.where(odd, mine, theirs)], axis=0)


def m_step(total, w_ref, bias_ref):
    classes = bias_ref.shape[0]
    feats = w_ref.shape[0] // classes
    groups = 128 // classes
    tiles = feats // groups
    lane, sub = iota((8, 128), 1), iota((8, 128), 0)
    group = lane // classes

    def rows(r):
        return total[r : r + 8]

    def spread_lanes(v, g):
        return jnp.take_along_axis(v, lane % classes + g * classes, axis=1, mode="promise_in_bounds")

    def spread_row(v, r):
        return jnp.broadcast_to(v[r : r + 1], (8, 128))

    base = tiles * feats
    counts = spread_lanes(spread_row(rows(base + feats), 0), 0)
    inv = 1.0 / counts
    means = [spread_lanes(rows(base + 8 * j), 0) / counts for j in range(tiles)]
    eye = jnp.where(sub == group, 1.0, 0.0)
    zero = jnp.zeros((8, 128), f32)
    mean_row = [
        jnp.broadcast_to(jnp.sum(eye * m, axis=0, keepdims=True), (8, 128)) for m in means
    ]
    mat = [
        [rows(t * feats + 8 * j) * inv - means[j] * mean_row[t] + (RIDGE * eye if t == j else 0.0) for t in range(tiles)]
        for j in range(tiles)
    ]
    side = [[eye if t == j else zero for t in range(tiles)] for j in range(tiles)] + [mean_row]
    diag = [zero] * tiles
    for p in range(0, feats, PIVOTS):
        at, g0 = p // 8, p % 8
        cols = [("m", j) for j in range(at, tiles)] + [("s", j) for j in (*range(at + 1), tiles)]
        held = {"m": mat, "s": side}
        head = [{(n, j): spread_lanes(held[n][j][at], g0 + s) for n, j in cols} for s in range(PIVOTS)]
        e = [[spread_row(head[s]["m", at], g0 + t) for t in range(PIVOTS)] for s in range(PIVOTS)]
        factors = [
            [spread_row(mat[at][t], g0 + s) if t >= at else None for t in range(tiles)] for s in range(PIVOTS)
        ]
        ells, scaled = {}, []
        for s in range(PIVOTS):
            r = 1.0 / e[s][s]
            for t in range(s + 1, PIVOTS):
                ells[s, t] = e[s][t] * r
                for c in cols:
                    head[t][c] = head[t][c] - ells[s, t] * head[s][c]
                for u in range(t, PIVOTS):
                    e[t][u] = e[t][u] - ells[s, t] * e[s][u]
            scaled.append({c: head[s][c] * r for c in cols})
        for s in reversed(range(PIVOTS)):
            for t in range(s + 1, PIVOTS):
                for c in cols:
                    scaled[s][c] = scaled[s][c] - ells[s, t] * scaled[t][c]
        for t in range(at, tiles):
            for s in range(PIVOTS):
                factor = factors[s][t]
                if t == at:
                    factor = jnp.where(group >= g0 + PIVOTS, factor, 0.0)
                for n, j in cols:
                    held[n][j][t] = held[n][j][t] - factor * scaled[s][n, j]
        for s in range(PIVOTS):
            own = group == g0 + s
            for n, j in cols:
                if n == "s":
                    side[j][at] = jnp.where(own, head[s][n, j], side[j][at])
            diag[at] = jnp.where(own, e[s][s], diag[at])
    logdet = sum(jnp.log(d) for d in diag)
    step = classes
    while step < 128:
        logdet = logdet + pltpu.roll(logdet, step, 1)
        step *= 2
    everything = jnp.sum(counts, axis=1, keepdims=True) * (1.0 / groups)
    bias = jnp.log(counts / everything) - 0.5 * logdet
    for t in range(tiles):
        scale = lax.rsqrt(diag[t])
        shift = -side[tiles][t] * scale
        high = shift.astype(bf16).astype(f32)
        middle = (shift - high).astype(bf16).astype(f32)
        low = shift - high - middle
        parts = jnp.where(sub == 0, high, jnp.where(sub == 1, middle, jnp.where(sub == 2, low, 0.0)))
        block = [side[j][t] * scale for j in range(tiles)] + [parts, zero, bias]
        turned = jnp.concatenate(block + [zero] * (16 - len(block)), axis=0).T
        w_ref[pl.ds(t * 128, 128), :] = turned[:, : feats + 16].astype(bf16)
        if t == 0:
            bias_ref[...] = jnp.broadcast_to(turned[:classes, feats + 16 : feats + 17], (classes, 128))
    return means


def loglik_of(x, w_ref, bias):
    parts = [loglik_part(x[j : j + VOXEL_ROWS], w_ref, bias) for j in range(0, x.shape[0], VOXEL_ROWS)]
    return jnp.concatenate(parts, axis=0)


def loglik_part(x, w_ref, bias):
    n, feats, nz = x.shape
    classes = bias.shape[0]
    xs = jnp.concatenate([x[j] for j in range(n)], axis=1)
    xs = jnp.concatenate([xs, jnp.ones((16, n * nz), bf16)], axis=0)
    white = jnp.dot(w_ref[...], xs, preferred_element_type=f32)
    white = white * white
    square = white[:classes]
    for g in range(1, feats):
        square = square + white[g * classes : (g + 1) * classes]
    return jnp.stack(
        [bias[:, :nz] - 0.5 * square[:, j * nz : (j + 1) * nz] for j in range(n)], axis=0
    )


def sharing(ny):
    return 128 // (2 * ny)


def own_lane(i, nx, ny, classes):
    start = 2 * ny * (i // (nx // sharing(ny)))
    lane, y = iota((ny, classes, 128), 2), iota((ny, classes, 128), 0)
    return (lane == start + y) | (lane == start + ny + y)


def shift_matrix(ny, nz):
    src, dst = iota((nz + 128, nz), 0), iota((nz + 128, nz), 1)
    near = (src < nz) & ((src == dst + 1) | (src == dst - 1))
    face = src - nz
    first = face % (2 * ny) < ny
    edge = (face >= 0) & ((first & (dst == nz - 1)) | (jnp.logical_not(first) & (dst == 0)))
    return jnp.where(near | edge, 1.0, 0.0).astype(bf16)


def take_matrix(ny, nz):
    src, dst = iota((nz, 128), 0), iota((nz, 128), 1)
    first = dst % (2 * ny) < ny
    hit = ((src == 0) & first) | ((src == nz - 1) & jnp.logical_not(first))
    return jnp.where(hit, 1.0, 0.0).astype(bf16)


def near_of(i, q_ref, y_halo, z_halo):
    nx, ny, classes, nz = q_ref.shape
    nx = nx - 2
    mid = q_ref[i + 1]
    down = q_ref[i].astype(f32)
    up = q_ref[i + 2].astype(f32)
    mid32 = mid.astype(f32)
    left = jnp.concatenate([y_halo[0, pl.ds(i, 1)], mid32[:-1]], axis=0)
    right = jnp.concatenate([mid32[1:], y_halo[1, pl.ds(i, 1)]], axis=0)
    face = z_halo[i % (nx // sharing(ny))]
    face = jnp.where(own_lane(i, nx, ny, classes), face[None], 0.0).astype(bf16)
    both = jnp.concatenate([mid, face], axis=2).reshape(ny * classes, nz + 128)
    along = jnp.dot(both, shift_matrix(ny, nz), preferred_element_type=f32)
    return (down + up) + (left + right) + along.reshape(ny, classes, nz)


def update_of(scores, near):
    s = scores + BETA * near
    e = jnp.exp(s - jnp.max(s, axis=1, keepdims=True))
    return (e * (1.0 / jnp.sum(e, axis=1, keepdims=True))).astype(bf16)


class Place:
    def __init__(self, place_ref, axis):
        self.sends, self.gets, self.before, self.after = (place_ref[4 * axis + j] for j in range(4))

    def halo(self, inner, outer):
        before = jnp.where(self.gets == 1, inner, outer)
        after = jnp.where(self.gets == 1, outer, inner)
        before = jnp.where(self.before == 1, before, 0.0)
        after = jnp.where(self.after == 1, after, 0.0)
        return before, after


def fill_halo(place_ref, halo, q_ref, padded, y_halo, z_halo):
    xi, xo, yi, yo, zi, zo = halo
    nx, ny, classes, nz = q_ref.shape
    before, after = Place(place_ref, 0).halo(xi[...].astype(f32), xo[...].astype(f32))
    padded[0], padded[nx + 1] = before.astype(bf16), after.astype(bf16)
    for i in range(nx):
        padded[i + 1] = q_ref[i]
    rows = y_halo.shape[1] * classes
    before, after = Place(place_ref, 1).halo(*(y[pl.ds(y.shape[0] - rows, rows), :] for y in (yi, yo)))
    y_halo[0], y_halo[1] = before.reshape(y_halo.shape[1:]), after.reshape(y_halo.shape[1:])
    rows = z_halo.shape[0] * classes
    before, after = Place(place_ref, 2).halo(*(z[pl.ds(z.shape[0] - rows, rows), :] for z in (zi, zo)))
    first = iota(before.shape, 1) % (2 * ny) < ny
    z_halo[...] = jnp.where(first, after, before).reshape(z_halo.shape)


def put_faces(place_ref, brick, xin, xout, yin, yout, zface):
    nx, ny, classes, nz = brick.shape
    first_in, first_in_y = Place(place_ref, 0).sends == 1, Place(place_ref, 1).sends == 1
    xin[...] = jnp.where(first_in, brick[0], brick[nx - 1])
    xout[...] = jnp.where(first_in, brick[nx - 1], brick[0])
    first = jnp.concatenate([brick[i, 0] for i in range(nx)], axis=0).astype(f32)
    last = jnp.concatenate([brick[i, ny - 1] for i in range(nx)], axis=0).astype(f32)
    rows = nx * classes
    yin[pl.ds(yin.shape[0] - rows, rows), :] = jnp.where(first_in_y, first, last)
    yout[...] = jnp.where(first_in_y, last, first)
    share = nx // sharing(ny)
    for j in range(share):
        total = None
        for i in range(j, nx, share):
            spread = jnp.dot(brick[i].reshape(ny * classes, nz), take_matrix(ny, nz), preferred_element_type=f32)
            spread = jnp.where(own_lane(i, nx, ny, classes), spread.reshape(ny, classes, 128), 0.0)
            spread = jnp.sum(spread, axis=0)
            total = spread if total is None else total + spread
        zface[pl.ds(j * classes, classes), :] = total


def over_slabs(nx, together, body, carry=None):
    def step(j, carry):
        for i in range(together):
            carry = body(j * together + i, carry)
        return carry

    if together == nx:
        return step(0, carry)
    return lax.fori_loop(0, nx // together, step, carry)


def all_near(near, space):
    def body(i, carry):
        near[i] = near_of(i, *space)
        return carry

    over_slabs(near.shape[0], TOGETHER["near"], body, 0)


def first_kernel(place, x_hbm, q_hbm, xt, qt, xin, xout, yout, zface, mine, theirs, x_in, q_in, sems):
    nx = xt.shape[0]
    feats, classes = xt.shape[2], qt.shape[2]

    def copies(i):
        return (
            pltpu.make_async_copy(q_hbm.at[:, i], q_in.at[i], sems.at[0, i]),
            pltpu.make_async_copy(x_hbm.at[:, i], x_in.at[i], sems.at[1, i]),
        )

    for i in range(nx):
        for copy in copies(i):
            copy.start()

    def slab(i, sums):
        for copy in copies(i):
            copy.wait()
        x = jnp.swapaxes(x_in[i], 0, 1)
        q = jnp.swapaxes(q_in[i], 0, 1)
        xt[i], qt[i] = x, q
        return jax.tree.map(jnp.add, sums, moments_of(x, q))

    sums = over_slabs(nx, TOGETHER["first"], slab, no_moments(feats, classes))
    put_faces(place, qt, xin, xout, theirs, yout, zface)
    put_moments(place, mine, theirs, *sums)


def second_kernel(
    place, mine, theirs, xt, qt, xi, xo, yi, yo, zi, zo, sc, q1, xin, xout, yin, yout, zface, w, bias, near, *space
):
    nx = xt.shape[0]
    fill_halo(place, (xi, xo, yi, yo, zi, zo), qt, *space)
    all_near(near, space)
    m_step(all_moments(place, mine, theirs), w, bias)

    def slab(i, carry):
        scores = loglik_of(xt[i], w, bias[...])
        sc[i] = scores
        q1[i] = update_of(scores, near[i])
        return carry

    over_slabs(nx, TOGETHER["second"], slab, 0)
    put_faces(place, q1, xin, xout, yin, yout, zface)


def third_kernel(place, sc, xt, qt, xi, xo, yi, yo, zi, zo, q2, xin, xout, yout, zface, mine, theirs, *space):
    nx = xt.shape[0]
    fill_halo(place, (xi, xo, yi, yo, zi, zo), qt, *space)

    def slab(i, sums):
        q = update_of(sc[i], near_of(i, *space))
        q2[i] = q
        return jax.tree.map(jnp.add, sums, moments_of(xt[i], q))

    sums = over_slabs(nx, TOGETHER["third"], slab, no_moments(xt.shape[2], qt.shape[2]))
    put_faces(place, q2, xin, xout, theirs, yout, zface)
    put_moments(place, mine, theirs, *sums)


def fourth_kernel(place, mine, theirs, xt, qt, xi, xo, yi, yo, zi, zo, seg, means_ref, w, bias, near, *space):
    nx = xt.shape[0]
    classes, feats = means_ref.shape
    fill_halo(place, (xi, xo, yi, yo, zi, zo), qt, *space)
    all_near(near, space)
    means = jnp.concatenate(m_step(all_moments(place, mine, theirs), w, bias), axis=0)
    means = jnp.concatenate([means, jnp.zeros((128 - feats, 128), f32)], axis=0).T
    means_ref[...] = means[:classes, :feats]

    def slab(i, carry):
        q = update_of(loglik_of(xt[i], w, bias[...]), near[i])
        seg[:, i] = jnp.swapaxes(q, 0, 1)
        return carry

    over_slabs(nx, TOGETHER["fourth"], slab, 0)


def pairings(n):
    if n == 2:
        return [[1, 0]]
    if n == 4:
        return [[1, 0, 3, 2], [3, 2, 1, 0], [2, 3, 0, 1]]
    return None


def send(value, axis, to):
    return lax.ppermute(value, axis, list(enumerate(to)))


def place_along(axis):
    n, at = lax.axis_size(axis), lax.axis_index(axis)
    if pairings(n) is None:
        return [0 * at, 0 * at + 1, at > 0, at < n - 1]
    return [at % 2, at % 2, at > 0, at < n - 1]


def send_middle(value, axis, other):
    n = lax.axis_size(other)
    if n % 2:
        return send(value, axis, pairings(4)[1])
    pairs = []
    for a in range(4):
        for o in range(n):
            here, there = (a, o), (3 - a, o) if a in (1, 2) else (a, o ^ 1)
            if axis == "gx":
                pairs.append((here[0] * n + here[1], there[0] * n + there[1]))
            else:
                pairs.append((here[1] * 4 + here[0], there[1] * 4 + there[0]))
    return lax.ppermute(value, ("gx", "gz"), pairs)


def swap(axis, inner, outer):
    n = lax.axis_size(axis)
    if n == 2:
        got = send(inner, axis, [1, 0])
        return got, got
    if n == 4:
        return send(inner, axis, pairings(n)[0]), send_middle(outer, axis, "gz" if axis == "gx" else "gx")
    return send(inner, axis, [(i + 1) % n for i in range(n)]), send(outer, axis, [(i - 1) % n for i in range(n)])


def exchange(xin, xout, yin, yout, zface):
    return *swap("gx", xin, xout), *swap("gy", yin, yout), *swap("gz", zface, zface)


def sum_and_exchange(xin, xout, yout, zface, mine, theirs):
    rows = mine.shape[0]
    paired = lax.axis_size("gy") == 2
    if paired:
        yi = yo = send(theirs, "gy", [1, 0])
        total = mine + yi[:rows]
    else:
        yi, yo = swap("gy", theirs[rows:], yout)
        total = lax.psum(jnp.concatenate([mine, theirs[:rows]], axis=0), "gy")
    if lax.axis_size("gx") == 4:
        total = sum((send(total, "gx", to) for to in pairings(4)), total)
    else:
        total = lax.psum(total, "gx")
    total, xin, xout = lax.optimization_barrier((total, xin, xout))
    xi, xo = swap("gx", xin, xout)
    if lax.axis_size("gz") == 4:
        n = total.shape[0]
        both = jnp.concatenate([total, zface], axis=0)
        zi, zo = (send(both, "gz", to) for to in pairings(4)[:2])
        total = total + zi[:n] + zo[:n] + send(total, "gz", pairings(4)[2])
    else:
        zi, zo = swap("gz", zface, zface)
        total = lax.psum(total, "gz")
    halves = (total, send(total, "gy", [1, 0])) if paired else (total[:rows], total[rows:])
    return *halves, xi, xo, yi, yo, zi, zo


def call(kernel, outs, scratch, places, *args, vmem=VMEM_BYTES):
    specs = [pl.BlockSpec(memory_space=place) for place in places]
    specs += [pl.BlockSpec(memory_space=pltpu.VMEM)] * (len(args) - len(places))
    return pl.pallas_call(
        kernel,
        out_shape=tuple(outs),
        in_specs=specs,
        out_specs=tuple(pl.BlockSpec(memory_space=pltpu.VMEM) for _ in outs),
        scratch_shapes=scratch,
        compiler_params=pltpu.CompilerParams(vmem_limit_bytes=vmem),
    )(*args)


class Sizes:
    def __init__(self, feats, classes, nx, ny, nz):
        shape = jax.ShapeDtypeStruct
        half = half_rows(feats, classes)
        share = nx // sharing(ny)
        self.features = shape((nx, ny, feats, nz), bf16)
        self.scores = shape((nx, ny, classes, nz), f32)
        self.brick = shape((nx, ny, classes, nz), bf16)
        self.face_x = shape((ny, classes, nz), bf16)
        self.face_y = shape((nx * classes, nz), f32)
        self.face_z = shape((share * classes, 128), f32)
        self.mine = shape((half, 128), f32)
        self.theirs = shape((half + nx * classes, 128), f32)
        self.out = shape((classes, nx, ny, nz), bf16)
        self.means = shape((classes, feats), f32)
        self.solved = [
            pltpu.VMEM((feats * classes, feats + 16), bf16),
            pltpu.VMEM((classes, 128), f32),
            pltpu.VMEM((nx, ny, classes, nz), f32),
        ]
        self.halos = [
            pltpu.VMEM((nx + 2, ny, classes, nz), bf16),
            pltpu.VMEM((2, nx, classes, nz), f32),
            pltpu.VMEM((share, classes, 128), f32),
        ]
        self.arrived = [
            pltpu.VMEM((nx, feats, ny, nz), bf16),
            pltpu.VMEM((nx, classes, ny, nz), bf16),
            pltpu.SemaphoreType.DMA((2, nx)),
        ]


def run_first(z, place, features, posteriors):
    outs = [z.features, z.brick, z.face_x, z.face_x, z.face_y, z.face_z, z.mine, z.theirs]
    places = [pltpu.SMEM, pltpu.HBM, pltpu.HBM]
    return call(first_kernel, outs, z.arrived, places, place, features, posteriors, vmem=48 * 2**20)


def run_second(z, place, mine, theirs, xt, qt, *halo):
    outs = [z.scores, z.brick, z.face_x, z.face_x, z.face_y, z.face_y, z.face_z]
    return call(second_kernel, outs, z.solved + z.halos, [pltpu.SMEM], place, mine, theirs, xt, qt, *halo)


def run_third(z, place, sc, xt, qt, *halo):
    outs = [z.brick, z.face_x, z.face_x, z.face_y, z.face_z, z.mine, z.theirs]
    return call(third_kernel, outs, z.halos, [pltpu.SMEM], place, sc, xt, qt, *halo)


def run_fourth(z, place, mine, theirs, xt, qt, *halo):
    return call(
        fourth_kernel, [z.out, z.means], z.solved + z.halos, [pltpu.SMEM], place, mine, theirs, xt, qt, *halo
    )


def local(features, posteriors):
    feats, nx, ny, nz = features.shape
    z = Sizes(feats, posteriors.shape[0], nx, ny, nz)
    place = jnp.stack([jnp.asarray(v, jnp.int32) for axis in AXES for v in place_along(axis)])
    xt, qt, *edge = run_first(z, place, features, posteriors)
    mine, theirs, *halo = sum_and_exchange(*edge)
    sc, q1, *edge = run_second(z, place, mine, theirs, xt, qt, *halo)
    halo = exchange(*edge)
    q2, *edge = run_third(z, place, sc, xt, q1, *halo)
    mine, theirs, *halo = sum_and_exchange(*edge)
    return run_fourth(z, place, mine, theirs, xt, q2, *halo)


def solution(mesh):
    placed = P(None, "gx", "gy", "gz")
    return jax.shard_map(
        local, mesh=mesh, in_specs=(placed, placed), out_specs=(placed, P()), check_vma=False
    )
```

```python
import jax
import jax.numpy as jnp
from jax import lax
from jax.experimental import pallas as pl
from jax.experimental.pallas import tpu as pltpu
from jax.sharding import PartitionSpec as P

BETA = 1.0
RIDGE = 0.1
AXES = ("gx", "gy", "gz")
ROWS_ROWS = (((1,), (1,)), ((), ()))
VMEM_BYTES = 36 * 2**20
PIVOTS = 8
VOXEL_ROWS = 8
CHUNK = 8
TOGETHER = {"first": 8, "near": 8, "second": 8, "third": 8, "fourth": 4}
f32, bf16 = jnp.float32, jnp.bfloat16


def iota(shape, dim):
    return lax.broadcasted_iota(jnp.int32, shape, dim)


def half_rows(feats, classes):
    return -(-(feats * feats * classes // 128 + feats + 8) // 16) * 8


def moments_of(x, q):
    ny, feats, _ = x.shape
    last = feats - 128 // q.shape[1]
    sums = None
    for c in range(0, ny, CHUNK):
        xs = jnp.concatenate([x[y] for y in range(c, c + CHUNK)], axis=1)
        qs = jnp.concatenate([q[y] for y in range(c, c + CHUNK)], axis=1)
        ones = jnp.ones((16, xs.shape[1]), bf16)
        weighted = [xs[f : f + 1] * qs for f in range(feats)]
        here = (
            lax.dot_general(xs, jnp.concatenate(weighted[:last], axis=0), ROWS_ROWS, preferred_element_type=f32),
            lax.dot_general(
                jnp.concatenate([*weighted[last:], qs], axis=0),
                jnp.concatenate([xs, ones], axis=0),
                ROWS_ROWS,
                preferred_element_type=f32,
            ),
        )
        sums = here if sums is None else jax.tree.map(jnp.add, sums, here)
    return sums


def no_moments(feats, classes):
    return jnp.zeros((feats, feats * classes - 128), f32), jnp.zeros((128 + classes, feats + 16), f32)


def put_moments(place_ref, mine, theirs, scatter, rest):
    feats, lanes = scatter.shape
    rows = [scatter[:, j : j + 128] for j in range(0, lanes, 128)]
    rest = jnp.pad(rest, ((0, 256 - rest.shape[0]), (0, 128 - rest.shape[1])))
    rows.append(rest[:128].T[:feats])
    rows.append(rest[128:].T[: feats + 8])
    half = mine.shape[0]
    rows.append(jnp.zeros((2 * half - sum(r.shape[0] for r in rows), 128), f32))
    rows = jnp.concatenate(rows, axis=0)
    odd = Place(place_ref, 1).sends == 1
    mine[...] = jnp.where(odd, rows[half:], rows[:half])
    theirs[pl.ds(0, half), :] = jnp.where(odd, rows[:half], rows[half:])


def all_moments(place_ref, mine, theirs):
    odd = Place(place_ref, 1).sends == 1
    mine, theirs = mine[...], theirs[...]
    return jnp.concatenate([jnp.where(odd, theirs, mine), jnp.where(odd, mine, theirs)], axis=0)


def m_step(total, w_ref, bias_ref):
    classes = bias_ref.shape[0]
    feats = w_ref.shape[0] // classes
    groups = 128 // classes
    tiles = feats // groups
    lane, sub = iota((8, 128), 1), iota((8, 128), 0)
    group = lane // classes

    def rows(r):
        return total[r : r + 8]

    def spread_lanes(v, g):
        return jnp.take_along_axis(v, lane % classes + g * classes, axis=1, mode="promise_in_bounds")

    def spread_row(v, r):
        return jnp.broadcast_to(v[r : r + 1], (8, 128))

    base = tiles * feats
    counts = spread_lanes(spread_row(rows(base + feats), 0), 0)
    inv = 1.0 / counts
    means = [spread_lanes(rows(base + 8 * j), 0) / counts for j in range(tiles)]
    eye = jnp.where(sub == group, 1.0, 0.0)
    zero = jnp.zeros((8, 128), f32)
    mean_row = [
        jnp.broadcast_to(jnp.sum(eye * m, axis=0, keepdims=True), (8, 128)) for m in means
    ]
    mat = [
        [rows(t * feats + 8 * j) * inv - means[j] * mean_row[t] + (RIDGE * eye if t == j else 0.0) for t in range(tiles)]
        for j in range(tiles)
    ]
    side = [[eye if t == j else zero for t in range(tiles)] for j in range(tiles)] + [mean_row]
    diag = [zero] * tiles
    for p in range(0, feats, PIVOTS):
        at, g0 = p // 8, p % 8
        cols = [("m", j) for j in range(at, tiles)] + [("s", j) for j in (*range(at + 1), tiles)]
        held = {"m": mat, "s": side}
        head = [{(n, j): spread_lanes(held[n][j][at], g0 + s) for n, j in cols} for s in range(PIVOTS)]
        e = [[spread_row(head[s]["m", at], g0 + t) for t in range(PIVOTS)] for s in range(PIVOTS)]
        factors = [
            [spread_row(mat[at][t], g0 + s) if t >= at else None for t in range(tiles)] for s in range(PIVOTS)
        ]
        ells, scaled = {}, []
        for s in range(PIVOTS):
            r = 1.0 / e[s][s]
            for t in range(s + 1, PIVOTS):
                ells[s, t] = e[s][t] * r
                for c in cols:
                    head[t][c] = head[t][c] - ells[s, t] * head[s][c]
                for u in range(t, PIVOTS):
                    e[t][u] = e[t][u] - ells[s, t] * e[s][u]
            scaled.append({c: head[s][c] * r for c in cols})
        for s in reversed(range(PIVOTS)):
            for t in range(s + 1, PIVOTS):
                for c in cols:
                    scaled[s][c] = scaled[s][c] - ells[s, t] * scaled[t][c]
        for t in range(at, tiles):
            for s in range(PIVOTS):
                factor = factors[s][t]
                if t == at:
                    factor = jnp.where(group >= g0 + PIVOTS, factor, 0.0)
                for n, j in cols:
                    held[n][j][t] = held[n][j][t] - factor * scaled[s][n, j]
        for s in range(PIVOTS):
            own = group == g0 + s
            for n, j in cols:
                if n == "s":
                    side[j][at] = jnp.where(own, head[s][n, j], side[j][at])
            diag[at] = jnp.where(own, e[s][s], diag[at])
    logdet = sum(jnp.log(d) for d in diag)
    step = classes
    while step < 128:
        logdet = logdet + pltpu.roll(logdet, step, 1)
        step *= 2
    everything = jnp.sum(counts, axis=1, keepdims=True) * (1.0 / groups)
    bias = jnp.log(counts / everything) - 0.5 * logdet
    for t in range(tiles):
        scale = lax.rsqrt(diag[t])
        shift = -side[tiles][t] * scale
        high = shift.astype(bf16).astype(f32)
        middle = (shift - high).astype(bf16).astype(f32)
        low = shift - high - middle
        parts = jnp.where(sub == 0, high, jnp.where(sub == 1, middle, jnp.where(sub == 2, low, 0.0)))
        block = [side[j][t] * scale for j in range(tiles)] + [parts, zero, bias]
        turned = jnp.concatenate(block + [zero] * (16 - len(block)), axis=0).T
        w_ref[pl.ds(t * 128, 128), :] = turned[:, : feats + 16].astype(bf16)
        if t == 0:
            bias_ref[...] = jnp.broadcast_to(turned[:classes, feats + 16 : feats + 17], (classes, 128))
    return means


def loglik_of(x, w_ref, bias):
    parts = [loglik_part(x[j : j + VOXEL_ROWS], w_ref, bias) for j in range(0, x.shape[0], VOXEL_ROWS)]
    return jnp.concatenate(parts, axis=0)


def loglik_part(x, w_ref, bias):
    n, feats, nz = x.shape
    classes = bias.shape[0]
    xs = jnp.concatenate([x[j] for j in range(n)], axis=1)
    xs = jnp.concatenate([xs, jnp.ones((16, n * nz), bf16)], axis=0)
    white = jnp.dot(w_ref[...], xs, preferred_element_type=f32)
    white = white * white
    square = white[:classes]
    for g in range(1, feats):
        square = square + white[g * classes : (g + 1) * classes]
    return jnp.stack(
        [bias[:, :nz] - 0.5 * square[:, j * nz : (j + 1) * nz] for j in range(n)], axis=0
    )


def sharing(ny):
    return 128 // (2 * ny)


def own_lane(i, nx, ny, classes):
    start = 2 * ny * (i // (nx // sharing(ny)))
    lane, y = iota((ny, classes, 128), 2), iota((ny, classes, 128), 0)
    return (lane == start + y) | (lane == start + ny + y)


def shift_matrix(ny, nz):
    src, dst = iota((nz + 128, nz), 0), iota((nz + 128, nz), 1)
    near = (src < nz) & ((src == dst + 1) | (src == dst - 1))
    face = src - nz
    first = face % (2 * ny) < ny
    edge = (face >= 0) & ((first & (dst == nz - 1)) | (jnp.logical_not(first) & (dst == 0)))
    return jnp.where(near | edge, 1.0, 0.0).astype(bf16)


def take_matrix(ny, nz):
    src, dst = iota((nz, 128), 0), iota((nz, 128), 1)
    first = dst % (2 * ny) < ny
    hit = ((src == 0) & first) | ((src == nz - 1) & jnp.logical_not(first))
    return jnp.where(hit, 1.0, 0.0).astype(bf16)


def near_of(i, q_ref, y_halo, z_halo):
    nx, ny, classes, nz = q_ref.shape
    nx = nx - 2
    mid = q_ref[i + 1]
    down = q_ref[i].astype(f32)
    up = q_ref[i + 2].astype(f32)
    mid32 = mid.astype(f32)
    left = jnp.concatenate([y_halo[0, pl.ds(i, 1)], mid32[:-1]], axis=0)
    right = jnp.concatenate([mid32[1:], y_halo[1, pl.ds(i, 1)]], axis=0)
    face = z_halo[i % (nx // sharing(ny))]
    face = jnp.where(own_lane(i, nx, ny, classes), face[None], 0.0).astype(bf16)
    both = jnp.concatenate([mid, face], axis=2).reshape(ny * classes, nz + 128)
    along = jnp.dot(both, shift_matrix(ny, nz), preferred_element_type=f32)
    return (down + up) + (left + right) + along.reshape(ny, classes, nz)


def update_of(scores, near):
    s = scores + BETA * near
    e = jnp.exp(s - jnp.max(s, axis=1, keepdims=True))
    return (e * (1.0 / jnp.sum(e, axis=1, keepdims=True))).astype(bf16)


class Place:
    def __init__(self, place_ref, axis):
        self.sends, self.gets, self.before, self.after = (place_ref[4 * axis + j] for j in range(4))

    def halo(self, inner, outer):
        before = jnp.where(self.gets == 1, inner, outer)
        after = jnp.where(self.gets == 1, outer, inner)
        before = jnp.where(self.before == 1, before, 0.0)
        after = jnp.where(self.after == 1, after, 0.0)
        return before, after


def fill_halo(place_ref, halo, q_ref, padded, y_halo, z_halo):
    xi, xo, yi, yo, zi, zo = halo
    nx, ny, classes, nz = q_ref.shape
    before, after = Place(place_ref, 0).halo(xi[...].astype(f32), xo[...].astype(f32))
    padded[0], padded[nx + 1] = before.astype(bf16), after.astype(bf16)
    for i in range(nx):
        padded[i + 1] = q_ref[i]
    rows = y_halo.shape[1] * classes
    before, after = Place(place_ref, 1).halo(*(y[pl.ds(y.shape[0] - rows, rows), :] for y in (yi, yo)))
    y_halo[0], y_halo[1] = before.reshape(y_halo.shape[1:]), after.reshape(y_halo.shape[1:])
    rows = z_halo.shape[0] * classes
    before, after = Place(place_ref, 2).halo(*(z[pl.ds(z.shape[0] - rows, rows), :] for z in (zi, zo)))
    first = iota(before.shape, 1) % (2 * ny) < ny
    z_halo[...] = jnp.where(first, after, before).reshape(z_halo.shape)


def put_faces(place_ref, brick, xin, xout, yin, yout, zface):
    nx, ny, classes, nz = brick.shape
    first_in, first_in_y = Place(place_ref, 0).sends == 1, Place(place_ref, 1).sends == 1
    xin[...] = jnp.where(first_in, brick[0], brick[nx - 1])
    xout[...] = jnp.where(first_in, brick[nx - 1], brick[0])
    first = jnp.concatenate([brick[i, 0] for i in range(nx)], axis=0).astype(f32)
    last = jnp.concatenate([brick[i, ny - 1] for i in range(nx)], axis=0).astype(f32)
    rows = nx * classes
    yin[pl.ds(yin.shape[0] - rows, rows), :] = jnp.where(first_in_y, first, last)
    yout[...] = jnp.where(first_in_y, last, first)
    share = nx // sharing(ny)
    for j in range(share):
        total = None
        for i in range(j, nx, share):
            spread = jnp.dot(brick[i].reshape(ny * classes, nz), take_matrix(ny, nz), preferred_element_type=f32)
            spread = jnp.where(own_lane(i, nx, ny, classes), spread.reshape(ny, classes, 128), 0.0)
            spread = jnp.sum(spread, axis=0)
            total = spread if total is None else total + spread
        zface[pl.ds(j * classes, classes), :] = total


def over_slabs(nx, together, body, carry=None):
    def step(j, carry):
        for i in range(together):
            carry = body(j * together + i, carry)
        return carry

    if together == nx:
        return step(0, carry)
    return lax.fori_loop(0, nx // together, step, carry)


def all_near(near, space):
    def body(i, carry):
        near[i] = near_of(i, *space)
        return carry

    over_slabs(near.shape[0], TOGETHER["near"], body, 0)


def first_kernel(place, x_hbm, q_hbm, xt, qt, xin, xout, yout, zface, mine, theirs, x_in, q_in, sems):
    nx = xt.shape[0]
    feats, classes = xt.shape[2], qt.shape[2]

    def copies(i):
        return (
            pltpu.make_async_copy(q_hbm.at[:, i], q_in.at[i], sems.at[0, i]),
            pltpu.make_async_copy(x_hbm.at[:, i], x_in.at[i], sems.at[1, i]),
        )

    for i in range(nx):
        for copy in copies(i):
            copy.start()

    def slab(i, sums):
        for copy in copies(i):
            copy.wait()
        x = jnp.swapaxes(x_in[i], 0, 1)
        q = jnp.swapaxes(q_in[i], 0, 1)
        xt[i], qt[i] = x, q
        return jax.tree.map(jnp.add, sums, moments_of(x, q))

    sums = over_slabs(nx, TOGETHER["first"], slab, no_moments(feats, classes))
    put_faces(place, qt, xin, xout, theirs, yout, zface)
    put_moments(place, mine, theirs, *sums)


def second_kernel(
    place, mine, theirs, xt, qt, xi, xo, yi, yo, zi, zo, sc, q1, xin, xout, yin, yout, zface, w, bias, near, *space
):
    nx = xt.shape[0]
    fill_halo(place, (xi, xo, yi, yo, zi, zo), qt, *space)
    all_near(near, space)
    m_step(all_moments(place, mine, theirs), w, bias)

    def slab(i, carry):
        scores = loglik_of(xt[i], w, bias[...])
        sc[i] = scores
        q1[i] = update_of(scores, near[i])
        return carry

    over_slabs(nx, TOGETHER["second"], slab, 0)
    put_faces(place, q1, xin, xout, yin, yout, zface)


def third_kernel(place, sc, xt, qt, xi, xo, yi, yo, zi, zo, q2, xin, xout, yout, zface, mine, theirs, *space):
    nx = xt.shape[0]
    fill_halo(place, (xi, xo, yi, yo, zi, zo), qt, *space)

    def slab(i, sums):
        q = update_of(sc[i], near_of(i, *space))
        q2[i] = q
        return jax.tree.map(jnp.add, sums, moments_of(xt[i], q))

    sums = over_slabs(nx, TOGETHER["third"], slab, no_moments(xt.shape[2], qt.shape[2]))
    put_faces(place, q2, xin, xout, theirs, yout, zface)
    put_moments(place, mine, theirs, *sums)


def fourth_kernel(place, mine, theirs, xt, qt, xi, xo, yi, yo, zi, zo, seg, means_ref, w, bias, near, *space):
    nx = xt.shape[0]
    classes, feats = means_ref.shape
    fill_halo(place, (xi, xo, yi, yo, zi, zo), qt, *space)
    all_near(near, space)
    means = jnp.concatenate(m_step(all_moments(place, mine, theirs), w, bias), axis=0)
    means = jnp.concatenate([means, jnp.zeros((128 - feats, 128), f32)], axis=0).T
    means_ref[...] = means[:classes, :feats]

    def slab(i, carry):
        q = update_of(loglik_of(xt[i], w, bias[...]), near[i])
        seg[:, i] = jnp.swapaxes(q, 0, 1)
        return carry

    over_slabs(nx, TOGETHER["fourth"], slab, 0)


def pairings(n):
    if n == 2:
        return [[1, 0]]
    if n == 4:
        return [[1, 0, 3, 2], [3, 2, 1, 0], [2, 3, 0, 1]]
    return None


def send(value, axis, to):
    return lax.ppermute(value, axis, list(enumerate(to)))


def place_along(axis):
    n, at = lax.axis_size(axis), lax.axis_index(axis)
    if pairings(n) is None:
        return [0 * at, 0 * at + 1, at > 0, at < n - 1]
    return [at % 2, at % 2, at > 0, at < n - 1]


def send_middle(value, axis, other):
    n = lax.axis_size(other)
    if n % 2:
        return send(value, axis, pairings(4)[1])
    pairs = []
    for a in range(4):
        for o in range(n):
            here, there = (a, o), (3 - a, o) if a in (1, 2) else (a, o ^ 1)
            if axis == "gx":
                pairs.append((here[0] * n + here[1], there[0] * n + there[1]))
            else:
                pairs.append((here[1] * 4 + here[0], there[1] * 4 + there[0]))
    return lax.ppermute(value, ("gx", "gz"), pairs)


def swap(axis, inner, outer):
    n = lax.axis_size(axis)
    if n == 2:
        got = send(inner, axis, [1, 0])
        return got, got
    if n == 4:
        return send(inner, axis, pairings(n)[0]), send_middle(outer, axis, "gz" if axis == "gx" else "gx")
    return send(inner, axis, [(i + 1) % n for i in range(n)]), send(outer, axis, [(i - 1) % n for i in range(n)])


def exchange(xin, xout, yin, yout, zface):
    return *swap("gx", xin, xout), *swap("gy", yin, yout), *swap("gz", zface, zface)


def sum_and_exchange(xin, xout, yout, zface, mine, theirs):
    rows = mine.shape[0]
    paired = lax.axis_size("gy") == 2
    if paired:
        yi = yo = send(theirs, "gy", [1, 0])
        total = mine + yi[:rows]
    else:
        yi, yo = swap("gy", theirs[rows:], yout)
        total = lax.psum(jnp.concatenate([mine, theirs[:rows]], axis=0), "gy")
    if lax.axis_size("gx") == 4:
        total = sum((send(total, "gx", to) for to in pairings(4)), total)
    else:
        total = lax.psum(total, "gx")
    total, xin, xout = lax.optimization_barrier((total, xin, xout))
    xi, xo = swap("gx", xin, xout)
    if lax.axis_size("gz") == 4:
        n = total.shape[0]
        both = jnp.concatenate([total, zface], axis=0)
        zi, zo = (send(both, "gz", to) for to in pairings(4)[:2])
        total = total + zi[:n] + zo[:n] + send(total, "gz", pairings(4)[2])
    else:
        zi, zo = swap("gz", zface, zface)
        total = lax.psum(total, "gz")
    halves = (total, send(total, "gy", [1, 0])) if paired else (total[:rows], total[rows:])
    return *halves, xi, xo, yi, yo, zi, zo


def call(kernel, outs, scratch, places, *args, vmem=VMEM_BYTES):
    specs = [pl.BlockSpec(memory_space=place) for place in places]
    specs += [pl.BlockSpec(memory_space=pltpu.VMEM)] * (len(args) - len(places))
    return pl.pallas_call(
        kernel,
        out_shape=tuple(outs),
        in_specs=specs,
        out_specs=tuple(pl.BlockSpec(memory_space=pltpu.VMEM) for _ in outs),
        scratch_shapes=scratch,
        compiler_params=pltpu.CompilerParams(vmem_limit_bytes=vmem),
    )(*args)


class Sizes:
    def __init__(self, feats, classes, nx, ny, nz):
        shape = jax.ShapeDtypeStruct
        half = half_rows(feats, classes)
        share = nx // sharing(ny)
        self.features = shape((nx, ny, feats, nz), bf16)
        self.scores = shape((nx, ny, classes, nz), f32)
        self.brick = shape((nx, ny, classes, nz), bf16)
        self.face_x = shape((ny, classes, nz), bf16)
        self.face_y = shape((nx * classes, nz), f32)
        self.face_z = shape((share * classes, 128), f32)
        self.mine = shape((half, 128), f32)
        self.theirs = shape((half + nx * classes, 128), f32)
        self.out = shape((classes, nx, ny, nz), bf16)
        self.means = shape((classes, feats), f32)
        self.solved = [
            pltpu.VMEM((feats * classes, feats + 16), bf16),
            pltpu.VMEM((classes, 128), f32),
            pltpu.VMEM((nx, ny, classes, nz), f32),
        ]
        self.halos = [
            pltpu.VMEM((nx + 2, ny, classes, nz), bf16),
            pltpu.VMEM((2, nx, classes, nz), f32),
            pltpu.VMEM((share, classes, 128), f32),
        ]
        self.arrived = [
            pltpu.VMEM((nx, feats, ny, nz), bf16),
            pltpu.VMEM((nx, classes, ny, nz), bf16),
            pltpu.SemaphoreType.DMA((2, nx)),
        ]


def run_first(z, place, features, posteriors):
    outs = [z.features, z.brick, z.face_x, z.face_x, z.face_y, z.face_z, z.mine, z.theirs]
    places = [pltpu.SMEM, pltpu.HBM, pltpu.HBM]
    return call(first_kernel, outs, z.arrived, places, place, features, posteriors, vmem=48 * 2**20)


def run_second(z, place, mine, theirs, xt, qt, *halo):
    outs = [z.scores, z.brick, z.face_x, z.face_x, z.face_y, z.face_y, z.face_z]
    return call(second_kernel, outs, z.solved + z.halos, [pltpu.SMEM], place, mine, theirs, xt, qt, *halo)


def run_third(z, place, sc, xt, qt, *halo):
    outs = [z.brick, z.face_x, z.face_x, z.face_y, z.face_z, z.mine, z.theirs]
    return call(third_kernel, outs, z.halos, [pltpu.SMEM], place, sc, xt, qt, *halo)


def run_fourth(z, place, mine, theirs, xt, qt, *halo):
    return call(
        fourth_kernel, [z.out, z.means], z.solved + z.halos, [pltpu.SMEM], place, mine, theirs, xt, qt, *halo
    )


def local(features, posteriors):
    feats, nx, ny, nz = features.shape
    z = Sizes(feats, posteriors.shape[0], nx, ny, nz)
    place = jnp.stack([jnp.asarray(v, jnp.int32) for axis in AXES for v in place_along(axis)])
    xt, qt, *edge = run_first(z, place, features, posteriors)
    mine, theirs, *halo = sum_and_exchange(*edge)
    sc, q1, *edge = run_second(z, place, mine, theirs, xt, qt, *halo)
    halo = exchange(*edge)
    q2, *edge = run_third(z, place, sc, xt, q1, *halo)
    mine, theirs, *halo = sum_and_exchange(*edge)
    return run_fourth(z, place, mine, theirs, xt, q2, *halo)


def solution(mesh):
    placed = P(None, "gx", "gy", "gz")
    return jax.shard_map(
        local, mesh=mesh, in_specs=(placed, placed), out_specs=(placed, P()), check_vma=False
    )
```

```python
import jax
import jax.numpy as jnp
from jax import lax
from jax.experimental import pallas as pl
from jax.experimental.pallas import tpu as pltpu
from jax.sharding import PartitionSpec as P

BETA = 1.0
RIDGE = 0.1
AXES = ("gx", "gy", "gz")
ROWS_ROWS = (((1,), (1,)), ((), ()))
VMEM_BYTES = 36 * 2**20
PIVOTS = 8
VOXEL_ROWS = 8
CHUNK = 8
TOGETHER = {"first": 8, "near": 8, "second": 8, "third": 8, "fourth": 4}
f32, bf16 = jnp.float32, jnp.bfloat16


def iota(shape, dim):
    return lax.broadcasted_iota(jnp.int32, shape, dim)


def half_rows(feats, classes):
    return -(-(feats * feats * classes // 128 + feats) // 16) * 8


def moments_of(x, q):
    ny, feats, _ = x.shape
    last = feats - 128 // q.shape[1]
    sums = None
    for c in range(0, ny, CHUNK):
        xs = jnp.concatenate([x[y] for y in range(c, c + CHUNK)], axis=1)
        qs = jnp.concatenate([q[y] for y in range(c, c + CHUNK)], axis=1)
        ones = jnp.ones((16, xs.shape[1]), bf16)
        weighted = [xs[f : f + 1] * qs for f in range(feats)]
        here = (
            lax.dot_general(xs, jnp.concatenate(weighted[:last], axis=0), ROWS_ROWS, preferred_element_type=f32),
            lax.dot_general(
                jnp.concatenate([*weighted[last:], qs], axis=0),
                jnp.concatenate([xs, ones], axis=0),
                ROWS_ROWS,
                preferred_element_type=f32,
            ),
        )
        sums = here if sums is None else jax.tree.map(jnp.add, sums, here)
    return sums


def no_moments(feats, classes):
    return jnp.zeros((feats, feats * classes - 128), f32), jnp.zeros((128 + classes, feats + 16), f32)


def put_moments(place_ref, mine, theirs, scatter, rest):
    feats, lanes = scatter.shape
    classes = rest.shape[0] - 128
    rows = [scatter[:, j : j + 128] for j in range(0, lanes, 128)]
    rest = jnp.pad(rest, ((0, 256 - rest.shape[0]), (0, 128 - rest.shape[1])))
    rows.append(rest[:128].T[:feats])
    first = rest[128:].T
    counts = pltpu.roll(first[feats : feats + 8], classes, 1)[:1]
    rows.append(first[:feats] + jnp.where(iota((feats, 128), 0) == 0, counts, 0.0))
    half = mine.shape[0]
    spare = 2 * half - sum(r.shape[0] for r in rows)
    if spare:
        rows.append(jnp.zeros((spare, 128), f32))
    rows = jnp.concatenate(rows, axis=0)
    odd = Place(place_ref, 1).sends == 1
    mine[...] = jnp.where(odd, rows[half:], rows[:half])
    theirs[pl.ds(0, half), :] = jnp.where(odd, rows[:half], rows[half:])


def all_moments(place_ref, mine, theirs):
    odd = Place(place_ref, 1).sends == 1
    mine, theirs = mine[...], theirs[...]
    return jnp.concatenate([jnp.where(odd, theirs, mine), jnp.where(odd, mine, theirs)], axis=0)


def m_step(total, w_ref, bias_ref):
    classes = bias_ref.shape[0]
    feats = w_ref.shape[0] // classes
    groups = 128 // classes
    tiles = feats // groups
    lane, sub = iota((8, 128), 1), iota((8, 128), 0)
    group = lane // classes

    def rows(r):
        return total[r : r + 8]

    def spread_lanes(v, g):
        return jnp.take_along_axis(v, lane % classes + g * classes, axis=1, mode="promise_in_bounds")

    def spread_row(v, r):
        return jnp.broadcast_to(v[r : r + 1], (8, 128))

    base = tiles * feats
    counts = spread_lanes(spread_row(rows(base), 0), 1)
    inv = 1.0 / counts
    means = [spread_lanes(rows(base + 8 * j), 0) / counts for j in range(tiles)]
    eye = jnp.where(sub == group, 1.0, 0.0)
    zero = jnp.zeros((8, 128), f32)
    mean_row = [
        jnp.broadcast_to(jnp.sum(eye * m, axis=0, keepdims=True), (8, 128)) for m in means
    ]
    mat = [
        [rows(t * feats + 8 * j) * inv - means[j] * mean_row[t] + (RIDGE * eye if t == j else 0.0) for t in range(tiles)]
        for j in range(tiles)
    ]
    side = [[eye if t == j else zero for t in range(tiles)] for j in range(tiles)] + [mean_row]
    diag = [zero] * tiles
    for p in range(0, feats, PIVOTS):
        at, g0 = p // 8, p % 8
        cols = [("m", j) for j in range(at, tiles)] + [("s", j) for j in (*range(at + 1), tiles)]
        held = {"m": mat, "s": side}
        head = [{(n, j): spread_lanes(held[n][j][at], g0 + s) for n, j in cols} for s in range(PIVOTS)]
        e = [[spread_row(head[s]["m", at], g0 + t) for t in range(PIVOTS)] for s in range(PIVOTS)]
        factors = [
            [spread_row(mat[at][t], g0 + s) if t >= at else None for t in range(tiles)] for s in range(PIVOTS)
        ]
        ells, scaled = {}, []
        for s in range(PIVOTS):
            r = 1.0 / e[s][s]
            for t in range(s + 1, PIVOTS):
                ells[s, t] = e[s][t] * r
                for c in cols:
                    head[t][c] = head[t][c] - ells[s, t] * head[s][c]
                for u in range(t, PIVOTS):
                    e[t][u] = e[t][u] - ells[s, t] * e[s][u]
            scaled.append({c: head[s][c] * r for c in cols})
        for s in reversed(range(PIVOTS)):
            for t in range(s + 1, PIVOTS):
                for c in cols:
                    scaled[s][c] = scaled[s][c] - ells[s, t] * scaled[t][c]
        for t in range(at, tiles):
            for s in range(PIVOTS):
                factor = factors[s][t]
                if t == at:
                    factor = jnp.where(group >= g0 + PIVOTS, factor, 0.0)
                for n, j in cols:
                    held[n][j][t] = held[n][j][t] - factor * scaled[s][n, j]
        for s in range(PIVOTS):
            own = group == g0 + s
            for n, j in cols:
                if n == "s":
                    side[j][at] = jnp.where(own, head[s][n, j], side[j][at])
            diag[at] = jnp.where(own, e[s][s], diag[at])
    logdet = sum(jnp.log(d) for d in diag)
    step = classes
    while step < 128:
        logdet = logdet + pltpu.roll(logdet, step, 1)
        step *= 2
    everything = jnp.sum(counts, axis=1, keepdims=True) * (1.0 / groups)
    bias = jnp.log(counts / everything) - 0.5 * logdet
    for t in range(tiles):
        scale = lax.rsqrt(diag[t])
        shift = -side[tiles][t] * scale
        high = shift.astype(bf16).astype(f32)
        middle = (shift - high).astype(bf16).astype(f32)
        low = shift - high - middle
        parts = jnp.where(sub == 0, high, jnp.where(sub == 1, middle, jnp.where(sub == 2, low, 0.0)))
        block = [side[j][t] * scale for j in range(tiles)] + [parts, zero, bias]
        turned = jnp.concatenate(block + [zero] * (16 - len(block)), axis=0).T
        w_ref[pl.ds(t * 128, 128), :] = turned[:, : feats + 16].astype(bf16)
        if t == 0:
            bias_ref[...] = jnp.broadcast_to(turned[:classes, feats + 16 : feats + 17], (classes, 128))
    return means


def loglik_of(x, w_ref, bias):
    parts = [loglik_part(x[j : j + VOXEL_ROWS], w_ref, bias) for j in range(0, x.shape[0], VOXEL_ROWS)]
    return jnp.concatenate(parts, axis=0)


def loglik_part(x, w_ref, bias):
    n, feats, nz = x.shape
    classes = bias.shape[0]
    xs = jnp.concatenate([x[j] for j in range(n)], axis=1)
    xs = jnp.concatenate([xs, jnp.ones((16, n * nz), bf16)], axis=0)
    white = jnp.dot(w_ref[...], xs, preferred_element_type=f32)
    white = white * white
    square = white[:classes]
    for g in range(1, feats):
        square = square + white[g * classes : (g + 1) * classes]
    return jnp.stack(
        [bias[:, :nz] - 0.5 * square[:, j * nz : (j + 1) * nz] for j in range(n)], axis=0
    )


def sharing(ny):
    return 128 // (2 * ny)


def own_lane(i, nx, ny, classes):
    start = 2 * ny * (i // (nx // sharing(ny)))
    lane, y = iota((ny, classes, 128), 2), iota((ny, classes, 128), 0)
    return (lane == start + y) | (lane == start + ny + y)


def shift_matrix(ny, nz):
    src, dst = iota((nz + 128, nz), 0), iota((nz + 128, nz), 1)
    near = (src < nz) & ((src == dst + 1) | (src == dst - 1))
    face = src - nz
    first = face % (2 * ny) < ny
    edge = (face >= 0) & ((first & (dst == nz - 1)) | (jnp.logical_not(first) & (dst == 0)))
    return jnp.where(near | edge, 1.0, 0.0).astype(bf16)


def take_matrix(ny, nz):
    src, dst = iota((nz, 128), 0), iota((nz, 128), 1)
    first = dst % (2 * ny) < ny
    hit = ((src == 0) & first) | ((src == nz - 1) & jnp.logical_not(first))
    return jnp.where(hit, 1.0, 0.0).astype(bf16)


def near_of(i, q_ref, y_halo, z_halo):
    nx, ny, classes, nz = q_ref.shape
    nx = nx - 2
    mid = q_ref[i + 1]
    down = q_ref[i].astype(f32)
    up = q_ref[i + 2].astype(f32)
    mid32 = mid.astype(f32)
    left = jnp.concatenate([y_halo[0, pl.ds(i, 1)], mid32[:-1]], axis=0)
    right = jnp.concatenate([mid32[1:], y_halo[1, pl.ds(i, 1)]], axis=0)
    face = z_halo[i % (nx // sharing(ny))]
    face = jnp.where(own_lane(i, nx, ny, classes), face[None], 0.0).astype(bf16)
    both = jnp.concatenate([mid, face], axis=2).reshape(ny * classes, nz + 128)
    along = jnp.dot(both, shift_matrix(ny, nz), preferred_element_type=f32)
    return (down + up) + (left + right) + along.reshape(ny, classes, nz)


def update_of(scores, near):
    s = scores + BETA * near
    e = jnp.exp(s - jnp.max(s, axis=1, keepdims=True))
    return (e * (1.0 / jnp.sum(e, axis=1, keepdims=True))).astype(bf16)


class Place:
    def __init__(self, place_ref, axis):
        self.sends, self.gets, self.before, self.after = (place_ref[4 * axis + j] for j in range(4))

    def halo(self, inner, outer):
        before = jnp.where(self.gets == 1, inner, outer)
        after = jnp.where(self.gets == 1, outer, inner)
        before = jnp.where(self.before == 1, before, 0.0)
        after = jnp.where(self.after == 1, after, 0.0)
        return before, after


def fill_halo(place_ref, halo, q_ref, padded, y_halo, z_halo):
    xi, xo, yi, yo, zi, zo = halo
    nx, ny, classes, nz = q_ref.shape
    before, after = Place(place_ref, 0).halo(xi[...].astype(f32), xo[...].astype(f32))
    padded[0], padded[nx + 1] = before.astype(bf16), after.astype(bf16)
    for i in range(nx):
        padded[i + 1] = q_ref[i]
    rows = y_halo.shape[1] * classes
    before, after = Place(place_ref, 1).halo(*(y[pl.ds(y.shape[0] - rows, rows), :] for y in (yi, yo)))
    y_halo[0], y_halo[1] = before.reshape(y_halo.shape[1:]), after.reshape(y_halo.shape[1:])
    rows = z_halo.shape[0] * classes
    before, after = Place(place_ref, 2).halo(*(z[pl.ds(z.shape[0] - rows, rows), :] for z in (zi, zo)))
    first = iota(before.shape, 1) % (2 * ny) < ny
    z_halo[...] = jnp.where(first, after, before).reshape(z_halo.shape)


def put_faces(place_ref, brick, xin, xout, yin, yout, zface):
    nx, ny, classes, nz = brick.shape
    first_in, first_in_y = Place(place_ref, 0).sends == 1, Place(place_ref, 1).sends == 1
    xin[...] = jnp.where(first_in, brick[0], brick[nx - 1])
    xout[...] = jnp.where(first_in, brick[nx - 1], brick[0])
    first = jnp.concatenate([brick[i, 0] for i in range(nx)], axis=0).astype(f32)
    last = jnp.concatenate([brick[i, ny - 1] for i in range(nx)], axis=0).astype(f32)
    rows = nx * classes
    yin[pl.ds(yin.shape[0] - rows, rows), :] = jnp.where(first_in_y, first, last)
    yout[...] = jnp.where(first_in_y, last, first)
    share = nx // sharing(ny)
    for j in range(share):
        total = None
        for i in range(j, nx, share):
            spread = jnp.dot(brick[i].reshape(ny * classes, nz), take_matrix(ny, nz), preferred_element_type=f32)
            spread = jnp.where(own_lane(i, nx, ny, classes), spread.reshape(ny, classes, 128), 0.0)
            spread = jnp.sum(spread, axis=0)
            total = spread if total is None else total + spread
        zface[pl.ds(j * classes, classes), :] = total


def over_slabs(nx, together, body, carry=None):
    def step(j, carry):
        for i in range(together):
            carry = body(j * together + i, carry)
        return carry

    if together == nx:
        return step(0, carry)
    return lax.fori_loop(0, nx // together, step, carry)


def all_near(near, space):
    def body(i, carry):
        near[i] = near_of(i, *space)
        return carry

    over_slabs(near.shape[0], TOGETHER["near"], body, 0)


def first_kernel(place, x_hbm, q_hbm, xt, qt, xin, xout, yout, zface, mine, theirs, x_in, q_in, sems):
    nx = xt.shape[0]
    feats, classes = xt.shape[2], qt.shape[2]

    def copies(i):
        return (
            pltpu.make_async_copy(q_hbm.at[:, i], q_in.at[i], sems.at[0, i]),
            pltpu.make_async_copy(x_hbm.at[:, i], x_in.at[i], sems.at[1, i]),
        )

    for i in range(nx):
        for copy in copies(i):
            copy.start()

    def slab(i, sums):
        for copy in copies(i):
            copy.wait()
        x = jnp.swapaxes(x_in[i], 0, 1)
        q = jnp.swapaxes(q_in[i], 0, 1)
        xt[i], qt[i] = x, q
        return jax.tree.map(jnp.add, sums, moments_of(x, q))

    sums = over_slabs(nx, TOGETHER["first"], slab, no_moments(feats, classes))
    put_faces(place, qt, xin, xout, theirs, yout, zface)
    put_moments(place, mine, theirs, *sums)


def second_kernel(
    place, mine, theirs, xt, qt, xi, xo, yi, yo, zi, zo, sc, q1, xin, xout, yin, yout, zface, w, bias, near, *space
):
    nx = xt.shape[0]
    fill_halo(place, (xi, xo, yi, yo, zi, zo), qt, *space)
    all_near(near, space)
    m_step(all_moments(place, mine, theirs), w, bias)

    def slab(i, carry):
        scores = loglik_of(xt[i], w, bias[...])
        sc[i] = scores
        q1[i] = update_of(scores, near[i])
        return carry

    over_slabs(nx, TOGETHER["second"], slab, 0)
    put_faces(place, q1, xin, xout, yin, yout, zface)


def third_kernel(place, sc, xt, qt, xi, xo, yi, yo, zi, zo, q2, xin, xout, yout, zface, mine, theirs, *space):
    nx = xt.shape[0]
    fill_halo(place, (xi, xo, yi, yo, zi, zo), qt, *space)

    def slab(i, sums):
        q = update_of(sc[i], near_of(i, *space))
        q2[i] = q
        return jax.tree.map(jnp.add, sums, moments_of(xt[i], q))

    sums = over_slabs(nx, TOGETHER["third"], slab, no_moments(xt.shape[2], qt.shape[2]))
    put_faces(place, q2, xin, xout, theirs, yout, zface)
    put_moments(place, mine, theirs, *sums)


def fourth_kernel(place, mine, theirs, xt, qt, xi, xo, yi, yo, zi, zo, seg, means_ref, w, bias, near, *space):
    nx = xt.shape[0]
    classes, feats = means_ref.shape
    fill_halo(place, (xi, xo, yi, yo, zi, zo), qt, *space)
    all_near(near, space)
    means = jnp.concatenate(m_step(all_moments(place, mine, theirs), w, bias), axis=0)
    means = jnp.concatenate([means, jnp.zeros((128 - feats, 128), f32)], axis=0).T
    means_ref[...] = means[:classes, :feats]

    def slab(i, carry):
        q = update_of(loglik_of(xt[i], w, bias[...]), near[i])
        seg[:, i] = jnp.swapaxes(q, 0, 1)
        return carry

    over_slabs(nx, TOGETHER["fourth"], slab, 0)


def pairings(n):
    if n == 2:
        return [[1, 0]]
    if n == 4:
        return [[1, 0, 3, 2], [3, 2, 1, 0], [2, 3, 0, 1]]
    return None


def send(value, axis, to):
    return lax.ppermute(value, axis, list(enumerate(to)))


def place_along(axis):
    n, at = lax.axis_size(axis), lax.axis_index(axis)
    if pairings(n) is None:
        return [0 * at, 0 * at + 1, at > 0, at < n - 1]
    return [at % 2, at % 2, at > 0, at < n - 1]


def send_middle(value, axis, other):
    n = lax.axis_size(other)
    if n % 2:
        return send(value, axis, pairings(4)[1])
    pairs = []
    for a in range(4):
        for o in range(n):
            here, there = (a, o), (3 - a, o) if a in (1, 2) else (a, o ^ 1)
            if axis == "gx":
                pairs.append((here[0] * n + here[1], there[0] * n + there[1]))
            else:
                pairs.append((here[1] * 4 + here[0], there[1] * 4 + there[0]))
    return lax.ppermute(value, ("gx", "gz"), pairs)


def swap(axis, inner, outer):
    n = lax.axis_size(axis)
    if n == 2:
        got = send(inner, axis, [1, 0])
        return got, got
    if n == 4:
        return send(inner, axis, pairings(n)[0]), send_middle(outer, axis, "gz" if axis == "gx" else "gx")
    return send(inner, axis, [(i + 1) % n for i in range(n)]), send(outer, axis, [(i - 1) % n for i in range(n)])


def exchange(xin, xout, yin, yout, zface):
    return *swap("gx", xin, xout), *swap("gy", yin, yout), *swap("gz", zface, zface)


def sum_and_exchange(xin, xout, yout, zface, mine, theirs):
    rows = mine.shape[0]
    paired = lax.axis_size("gy") == 2
    if paired:
        yi = yo = send(theirs, "gy", [1, 0])
        total = mine + yi[:rows]
    else:
        yi, yo = swap("gy", theirs[rows:], yout)
        total = lax.psum(jnp.concatenate([mine, theirs[:rows]], axis=0), "gy")
    if lax.axis_size("gx") == 4:
        total = sum((send(total, "gx", to) for to in pairings(4)), total)
    else:
        total = lax.psum(total, "gx")
    total, xin, xout = lax.optimization_barrier((total, xin, xout))
    xi, xo = swap("gx", xin, xout)
    if lax.axis_size("gz") == 4:
        n = total.shape[0]
        both = jnp.concatenate([total, zface], axis=0)
        zi, zo = (send(both, "gz", to) for to in pairings(4)[:2])
        total = total + zi[:n] + zo[:n] + send(total, "gz", pairings(4)[2])
    else:
        zi, zo = swap("gz", zface, zface)
        total = lax.psum(total, "gz")
    halves = (total, send(total, "gy", [1, 0])) if paired else (total[:rows], total[rows:])
    return *halves, xi, xo, yi, yo, zi, zo


def call(kernel, outs, scratch, places, *args, vmem=VMEM_BYTES):
    specs = [pl.BlockSpec(memory_space=place) for place in places]
    specs += [pl.BlockSpec(memory_space=pltpu.VMEM)] * (len(args) - len(places))
    return pl.pallas_call(
        kernel,
        out_shape=tuple(outs),
        in_specs=specs,
        out_specs=tuple(pl.BlockSpec(memory_space=pltpu.VMEM) for _ in outs),
        scratch_shapes=scratch,
        compiler_params=pltpu.CompilerParams(vmem_limit_bytes=vmem),
    )(*args)


class Sizes:
    def __init__(self, feats, classes, nx, ny, nz):
        shape = jax.ShapeDtypeStruct
        half = half_rows(feats, classes)
        share = nx // sharing(ny)
        self.features = shape((nx, ny, feats, nz), bf16)
        self.scores = shape((nx, ny, classes, nz), f32)
        self.brick = shape((nx, ny, classes, nz), bf16)
        self.face_x = shape((ny, classes, nz), bf16)
        self.face_y = shape((nx * classes, nz), f32)
        self.face_z = shape((share * classes, 128), f32)
        self.mine = shape((half, 128), f32)
        self.theirs = shape((half + nx * classes, 128), f32)
        self.out = shape((classes, nx, ny, nz), bf16)
        self.means = shape((classes, feats), f32)
        self.solved = [
            pltpu.VMEM((feats * classes, feats + 16), bf16),
            pltpu.VMEM((classes, 128), f32),
            pltpu.VMEM((nx, ny, classes, nz), f32),
        ]
        self.halos = [
            pltpu.VMEM((nx + 2, ny, classes, nz), bf16),
            pltpu.VMEM((2, nx, classes, nz), f32),
            pltpu.VMEM((share, classes, 128), f32),
        ]
        self.arrived = [
            pltpu.VMEM((nx, feats, ny, nz), bf16),
            pltpu.VMEM((nx, classes, ny, nz), bf16),
            pltpu.SemaphoreType.DMA((2, nx)),
        ]


def run_first(z, place, features, posteriors):
    outs = [z.features, z.brick, z.face_x, z.face_x, z.face_y, z.face_z, z.mine, z.theirs]
    places = [pltpu.SMEM, pltpu.HBM, pltpu.HBM]
    return call(first_kernel, outs, z.arrived, places, place, features, posteriors, vmem=48 * 2**20)


def run_second(z, place, mine, theirs, xt, qt, *halo):
    outs = [z.scores, z.brick, z.face_x, z.face_x, z.face_y, z.face_y, z.face_z]
    return call(second_kernel, outs, z.solved + z.halos, [pltpu.SMEM], place, mine, theirs, xt, qt, *halo)


def run_third(z, place, sc, xt, qt, *halo):
    outs = [z.brick, z.face_x, z.face_x, z.face_y, z.face_z, z.mine, z.theirs]
    return call(third_kernel, outs, z.halos, [pltpu.SMEM], place, sc, xt, qt, *halo)


def run_fourth(z, place, mine, theirs, xt, qt, *halo):
    return call(
        fourth_kernel, [z.out, z.means], z.solved + z.halos, [pltpu.SMEM], place, mine, theirs, xt, qt, *halo
    )


def local(features, posteriors):
    feats, nx, ny, nz = features.shape
    z = Sizes(feats, posteriors.shape[0], nx, ny, nz)
    place = jnp.stack([jnp.asarray(v, jnp.int32) for axis in AXES for v in place_along(axis)])
    xt, qt, *edge = run_first(z, place, features, posteriors)
    mine, theirs, *halo = sum_and_exchange(*edge)
    sc, q1, *edge = run_second(z, place, mine, theirs, xt, qt, *halo)
    halo = exchange(*edge)
    q2, *edge = run_third(z, place, sc, xt, q1, *halo)
    mine, theirs, *halo = sum_and_exchange(*edge)
    return run_fourth(z, place, mine, theirs, xt, q2, *halo)


def solution(mesh):
    placed = P(None, "gx", "gy", "gz")
    return jax.shard_map(
        local, mesh=mesh, in_specs=(placed, placed), out_specs=(placed, P()), check_vma=False
    )
```
